32 devices in a mesh: groups: 2 (over y), tok: 4 (over z), head: 4 (over x, core).
Axes of the slice: x: 2, y: 2, z: 4, core: 2. Of those that a mesh axis runs over, the one named last changes fastest.
Arguments:
- queries: bfloat16 [2048, 2048], P(('groups', 'tok'), 'head'), parts along dimension 0, may hold values from -8 to 8
- keys: bfloat16 [2048, 2048], P(('groups', 'tok'), 'head'), parts along dimension 0, may hold values from -8 to 8
- values: bfloat16 [2048, 2048], P(('groups', 'tok'), 'head'), parts along dimension 0, may hold values from -8 to 8
- fast_in: bfloat16 [4, 512, 1024], P('head'), may hold values from -0.25 to 0.25
- fast_out: bfloat16 [4, 512, 512], P('head'), may hold values from -0.25 to 0.25
- key_gain: float32 [4], P('head'), may hold values from 0.35 to 1.4
- out_proj: bfloat16 [2048, 4096], P('head', 'tok'), may hold values from -2 to 2
- grad_out: bfloat16 [2048, 4096], P(('groups', 'tok')), parts along dimension 0, may hold values from -12 to 12
Outputs:
- d_queries: bfloat16 [2048, 2048], P(('groups', 'tok'), 'head'), parts along dimension 0
- d_keys: bfloat16 [2048, 2048], P(('groups', 'tok'), 'head'), parts along dimension 0
- d_values: bfloat16 [2048, 2048], P(('groups', 'tok'), 'head'), parts along dimension 0
The draws below stay inside these ranges and needn't reach their ends.
There are 2 independent parts, one for each index of `groups`. The reference program is written for one: setup_inputs(seed, part) draws one part's arguments, and reference() takes and returns one part's arrays. A program takes and returns all parts, laid end to end along the dimension named above; an argument that names none is the same for every part. Nothing has to cross between parts.
All inputs are finite; a program needn't handle non-finite values.
Results may differ from the reference program's by a relative error of at most 0.0012.
Values may be sent and summed in bfloat16 or wider, within the bound.
No kernel may reach another device: no remote copies, remote signals or barrier semaphores. Data moves between devices by JAX's collectives and lax.ppermute only.
A program may use at most 64 MiB of HBM per device.

```python
import math
from functools import partial
import jax
import jax.numpy as jnp
from jax import lax

D = 4096
HD = 512
HH = 512
HEADS = 4
TOKENS = 1024


def shaped_field(key, width):
    parts = jax.random.split(key, 1)
    normal = jnp.clip(jax.random.normal(parts[0], (TOKENS, width), jnp.float32), -4.0, 4.0)
    mixed = normal
    return mixed


def token_fields(key):
    parts = jax.random.split(key, 2)
    key_field = shaped_field(parts[0], HEADS * HD)
    value_field = shaped_field(parts[1], HEADS * HD)
    return (key_field, value_field)


def draw_keys(key, part):
    key_field, value_field = token_fields(key)
    return jnp.clip(key_field, -8.0, 8.0).astype(jnp.bfloat16)


def draw_values(key, part):
    key_field, value_field = token_fields(key)
    return jnp.clip(value_field, -8.0, 8.0).astype(jnp.bfloat16)


def draw_queries(key, part):
    key_field, value_field = token_fields(key)
    own_key = jax.random.fold_in(key, 3)
    noise = shaped_field(own_key, HEADS * HD)
    return jnp.clip(0.85 * key_field + 0.53 * noise, -8.0, 8.0).astype(jnp.bfloat16)


def draw_grad_out(key, part):
    key_field, value_field = token_fields(key)
    own_key = jax.random.fold_in(key, 7)
    noise = shaped_field(own_key, D)
    period = min(D, HEADS * HD)
    groups_in = HEADS * HD // period
    targets = jnp.clip(value_field, -8.0, 8.0)
    folded = targets.reshape(TOKENS, groups_in, period).sum(axis=1)
    spread = jnp.tile(folded, (1, D // period))
    return jnp.clip(0.6 * noise - spread, -12.0, 12.0).astype(jnp.bfloat16)


def draw_out_proj(key, part):
    key = jax.random.fold_in(key, 5)
    period = min(D, HEADS * HD)
    row_ids = jnp.arange(HEADS * HD, dtype=jnp.int32)[:, None] % period
    col_ids = jnp.arange(D, dtype=jnp.int32)[None, :] % period
    pattern = (row_ids == col_ids).astype(jnp.float32)
    noise = jnp.clip(jax.random.normal(key, (HEADS * HD, D), jnp.float32), -4.0, 4.0)
    return jnp.clip(pattern + 0.8 * noise / math.sqrt(D), -2.0, 2.0).astype(jnp.bfloat16)


def steps_of(rng, shape, pieces, low, top_value):
    level = 1.0
    for position, blocks in pieces:
        draws = jax.random.uniform(jax.random.fold_in(jax.random.fold_in(rng, 6), position), (blocks,), jnp.float32, low / len(pieces), top_value / len(pieces))
        level = level * jnp.repeat(jnp.exp(draws), shape[position] // blocks).reshape((-1,) + (1,) * (len(shape) - 1 - position))
    return level


def centred(key, extent, scale, reach, cuts=(), held_as=jnp.bfloat16):
    values = jax.random.normal(key, extent, jnp.float32) * scale
    if len(cuts) > 0:
        values = steps_of(key, extent, cuts, -0.22, 0.18) * values
    return jnp.clip(values, min=-reach, max=reach).astype(held_as)


def setup_inputs(seed: int = 0, part: int = 0) -> dict:
    key_list = jax.random.split(jax.random.key(seed), 9)
    part_splits = jax.random.split(jax.random.fold_in(key_list[8], part), 9)
    queries = draw_queries(jax.random.fold_in(jax.random.fold_in(key_list[8], part), 71), part)
    keys = draw_keys(jax.random.fold_in(jax.random.fold_in(key_list[8], part), 71), part)
    values = draw_values(jax.random.fold_in(jax.random.fold_in(key_list[8], part), 71), part)
    fast_in = centred(key_list[3], (HEADS, HD, 2 * HH), HD ** -0.5, 0.25, ((0, 4),))
    fast_out = centred(key_list[4], (HEADS, HH, HD), HH ** -0.5, 0.25, ((0, 4),))
    key_gain = jnp.clip(jnp.exp(math.log(1.4) - 1.3862944 * jax.random.uniform(key_list[5], (HEADS,), jnp.float32) ** steps_of(key_list[5], (HEADS,), ((0, 4),), -0.2, 0.2)), 0.35, 1.4)
    out_proj = draw_out_proj(jax.random.fold_in(key_list[8], 71), part)
    grad_out = draw_grad_out(jax.random.fold_in(jax.random.fold_in(key_list[8], part), 71), part)
    return {"queries": queries, "keys": keys, "values": values, "fast_in": fast_in, "fast_out": fast_out, "key_gain": key_gain, "out_proj": out_proj, "grad_out": grad_out}


highest = lax.Precision.HIGHEST
inner_rate = 0.02
norm_eps = 1e-06

def fast_apply(weights, inputs):
    w_both, w_down = weights
    half_width = w_down.shape[0]
    mixed = jnp.dot(inputs, w_both, precision=highest)
    hidden = jax.nn.silu(mixed[:, :half_width]) * mixed[:, half_width:]
    return jnp.dot(hidden, w_down, precision=highest)

def inner_loss(weights, inputs, targets):
    misfit = fast_apply(weights, inputs) - targets
    return 0.5 * jnp.sum(misfit * misfit)

def inner_grad(weights, inputs, targets):
    return jax.grad(inner_loss)(weights, inputs, targets)

def query_pull(weights, inputs, cotangent):
    _, pullback = jax.vjp(fast_apply, weights, inputs)
    return pullback(cotangent)

def key_pull(weights, inputs, targets, cotangent):
    _, pullback = jax.vjp(partial(inner_grad, weights), inputs, targets)
    return pullback(cotangent)

def split_heads(array, heads):
    return array.reshape(array.shape[0], heads, -1).transpose(1, 0, 2).astype(jnp.float32)

def join_heads(array):
    return array.transpose(1, 0, 2).reshape(array.shape[1], -1).astype(jnp.bfloat16)

def frobenius(former, latter):
    return jnp.sum(former[0] * latter[0]) + jnp.sum(former[1] * latter[1])

def reference(queries, keys, values, fast_in, fast_out, key_gain, out_proj, grad_out):
    heads = key_gain.shape[0]
    gain_col = key_gain.astype(jnp.float32)[:, None, None]
    query_heads = split_heads(queries, heads)
    key_heads = split_heads(keys, heads) * gain_col
    value_heads = split_heads(values, heads)
    weights = (fast_in.astype(jnp.float32), fast_out.astype(jnp.float32))
    full_grad = jax.vmap(inner_grad)(weights, key_heads, value_heads)
    entries = full_grad[0].size + full_grad[1].size
    grad_rms = jnp.sqrt(frobenius(full_grad, full_grad) / entries)
    denom = grad_rms + norm_eps
    updated = tuple((member_w - inner_rate * member_g / denom for member_w, member_g in zip(weights, full_grad)))
    out_grad = jnp.dot(grad_out, out_proj.T, preferred_element_type=jnp.float32)
    out_heads = split_heads(out_grad, heads)
    adjoint, query_grad = jax.vmap(query_pull)(updated, query_heads, out_heads)
    product = frobenius(full_grad, adjoint)
    grad_adjoint = tuple((-inner_rate * (member_a / denom - member_g * product / (denom * denom * entries * grad_rms)) for member_a, member_g in zip(adjoint, full_grad)))
    key_grad, value_grad = jax.vmap(key_pull)(weights, key_heads, value_heads, grad_adjoint)
    return (join_heads(query_grad), join_heads(key_grad * gain_col), join_heads(value_grad))
```

```python
from functools import partial

import jax
import jax.numpy as jnp
from jax import lax
from jax.experimental import pallas as pl
from jax.experimental.pallas import tpu as pltpu
from jax.sharding import PartitionSpec as P

f32 = jnp.float32
bf16 = jnp.bfloat16
inner_rate = 0.02
norm_eps = 1e-06
vmem_bytes = 56 * 1024 * 1024
MIB = 1024 * 1024


def halves(x):
    top = x.astype(bf16)
    return top, (x - top.astype(f32)).astype(bf16)


def nn(a, b):
    return lax.dot_general(a, b, (((1,), (0,)), ((), ())), preferred_element_type=f32)


def nt(a, b):
    return lax.dot_general(a, b, (((1,), (1,)), ((), ())), preferred_element_type=f32)


def tn(a, b):
    return lax.dot_general(a, b, (((0,), (0,)), ((), ())), preferred_element_type=f32)


def two(dot, a, b):
    return dot(a[0], b) + dot(a[1], b)


def two_right(dot, a, b):
    return dot(a, b[0]) + dot(a, b[1])


def three(dot, a, b):
    return dot(a[0], b[0]) + dot(a[0], b[1]) + dot(a[1], b[0])


def sigmoid(u):
    return 1.0 / (1.0 + jnp.exp(-u))


def fetch_all(slots, held, sems):
    for j, slot in enumerate(slots):
        pltpu.make_async_copy(slot, held.at[j], sems.at[j]).start()


def inner_grad_kernel(count, keep, *refs):
    slots = refs[:count]
    gain_ref, wa_ref, wb_ref, ga_ref, gb_ref, sq_ref = refs[count : count + 6]
    held, sems = refs[-2:]
    fetch_all(slots, held, sems)
    gain = gain_ref[0]
    width = wb_ref.shape[0]
    ga_ref[...] = jnp.zeros_like(ga_ref)
    gb_ref[...] = jnp.zeros_like(gb_ref)

    @pl.loop(0, count)
    def _(j):
        pltpu.make_async_copy(slots[0], held.at[j], sems.at[j]).wait()
        keys = held[j, :, :width]
        values = held[j, :, width : 2 * width].astype(f32)
        mixed = nn(keys, wa_ref[...]) * gain
        u, w = mixed[:, :width], mixed[:, width:]
        sg = sigmoid(u)
        act = u * sg
        hidden = halves(act * w)
        e = two(nn, hidden, wb_ref[...]) - values
        e2 = halves(e)
        hb = two(nt, e2, wb_ref[...])
        if keep:
            e_ref, hb_ref = refs[count + 6 : count + 8]
            e_ref[j] = e
            hb_ref[j] = hb
        gb_ref[...] += three(tn, hidden, e2)
        slope = sg * (1.0 + u * (1.0 - sg))
        ga_ref[:, :width] += two_right(tn, keys, halves(hb * w * slope))
        ga_ref[:, width:] += two_right(tn, keys, halves(hb * act))

    ga = ga_ref[...] * gain
    ga_ref[...] = ga
    gb = gb_ref[...]
    sq_ref[...] = jnp.zeros_like(sq_ref) + (jnp.sum(ga * ga) + jnp.sum(gb * gb))


def vmem_spec():
    return pl.BlockSpec(memory_space=pltpu.VMEM)


def any_spec():
    return pl.BlockSpec(memory_space=pl.ANY)


def smem_spec():
    return pl.BlockSpec(memory_space=pltpu.SMEM)


def shape_of(*dims, dtype=f32):
    return jax.ShapeDtypeStruct(dims, dtype)


def estimate(units, rows):
    return pl.CostEstimate(
        flops=units * 2 * rows * 512 * 512, bytes_accessed=8 * MIB, transcendentals=0
    )


def call_inner_grad(slots, keep, gain, wa, wb):
    count = len(slots)
    kept = 2 if keep else 0
    rows, width = slots[0].shape[0], wb.shape[0]
    return pl.pallas_call(
        partial(inner_grad_kernel, count, keep),
        out_shape=(shape_of(width, 2 * width), shape_of(width, width), shape_of(8, 128))
        + (shape_of(count, rows, width),) * kept,
        in_specs=[any_spec()] * count + [smem_spec(), vmem_spec(), vmem_spec()],
        out_specs=[vmem_spec()] * (3 + kept),
        scratch_shapes=[
            pltpu.VMEM((count,) + slots[0].shape, bf16),
            pltpu.SemaphoreType.DMA((count,)),
        ],
        compiler_params=pltpu.CompilerParams(vmem_limit_bytes=vmem_bytes),
        cost_estimate=estimate(13, rows * count),
        name="inner_grad",
    )(*slots, gain, wa, wb)


def scale_of(sums, entries):
    total = sums[0][0:1, 0:1]
    for more in sums[1:]:
        total = total + more[0:1, 0:1]
    rms = jnp.sqrt(total / entries)
    return rms, rms + norm_eps


def query_kernel(count, n_sums, entries, swap, *refs):
    slots, refs = refs[:count], refs[count:]
    own, refs = refs[:count], refs[count:]
    other, refs = refs[:count], refs[count:]
    sums, refs = refs[:n_sums], refs[n_sums:]
    (wa_ref, wb_ref, ga_ref, gb_ref), refs = refs[:4], refs[4:]
    (da_ref, db_ref, p_ref), refs = refs[:3], refs[3:]
    dq, refs = refs[:count], refs[count:]
    held, left, right, ah, al, bh, bl, dq_held, sem_q, sem_l, sem_r, sem_o = refs
    width = wb_ref.shape[0]
    for j in range(count):
        pltpu.make_async_copy(
            slots[j].at[:, 2 * width : 3 * width], held.at[j], sem_q.at[j]
        ).start()
        pltpu.make_async_copy(own[j], left.at[j], sem_l.at[j]).start()
        pltpu.make_async_copy(other[swap[j]], right.at[j], sem_r.at[j]).start()
    _, scale = scale_of(sums, entries)
    rate = inner_rate / scale
    ah[...], al[...] = halves(wa_ref[...].astype(f32) - ga_ref[...] * rate)
    bh[...], bl[...] = halves(wb_ref[...].astype(f32) - gb_ref[...] * rate)
    da_ref[...] = jnp.zeros_like(da_ref)
    db_ref[...] = jnp.zeros_like(db_ref)

    @pl.loop(0, count)
    def _(j):
        pltpu.make_async_copy(
            slots[0].at[:, 2 * width : 3 * width], held.at[j], sem_q.at[j]
        ).wait()
        pltpu.make_async_copy(own[0], left.at[j], sem_l.at[j]).wait()
        pltpu.make_async_copy(other[0], right.at[j], sem_r.at[j]).wait()
        queries = held[j]
        d_out = halves(left[j] + right[j])
        a = (ah[...], al[...])
        b = (bh[...], bl[...])
        mixed = two_right(nn, queries, a)
        u, w = mixed[:, :width], mixed[:, width:]
        sg = sigmoid(u)
        act = u * sg
        hb = three(nt, d_out, b)
        db_ref[...] += three(tn, halves(act * w), d_out)
        slope = sg * (1.0 + u * (1.0 - sg))
        ub = halves(hb * w * slope)
        wbar = halves(hb * act)
        da_ref[:, :width] += two_right(tn, queries, ub)
        da_ref[:, width:] += two_right(tn, queries, wbar)
        back = three(nt, ub, (ah[:, :width], al[:, :width])) + three(
            nt, wbar, (ah[:, width:], al[:, width:])
        )
        dq_held[j] = back.astype(bf16)

    copies = [pltpu.make_async_copy(dq_held.at[j], dq[j], sem_o.at[j]) for j in range(count)]
    for copy in copies:
        copy.start()
    total = jnp.sum(ga_ref[...] * da_ref[...]) + jnp.sum(gb_ref[...] * db_ref[...])
    p_ref[...] = jnp.zeros_like(p_ref) + total
    for copy in copies:
        copy.wait()


def call_query(slots, own, other, swap, sums, entries, wa, wb, ga, gb):
    count = len(slots)
    rows, width = slots[0].shape[0], wb.shape[0]
    outs = pl.pallas_call(
        partial(query_kernel, count, len(sums), entries, swap),
        out_shape=(shape_of(width, 2 * width), shape_of(width, width), shape_of(8, 128))
        + (shape_of(rows, width, dtype=bf16),) * count,
        in_specs=[any_spec()] * (3 * count) + [vmem_spec()] * (len(sums) + 4),
        out_specs=[vmem_spec()] * 3 + [any_spec()] * count,
        scratch_shapes=[
            pltpu.VMEM((count, rows, width), bf16),
            pltpu.VMEM((count, rows, width), f32),
            pltpu.VMEM((count, rows, width), f32),
            pltpu.VMEM((width, 2 * width), bf16),
            pltpu.VMEM((width, 2 * width), bf16),
            pltpu.VMEM((width, width), bf16),
            pltpu.VMEM((width, width), bf16),
            pltpu.VMEM((count, rows, width), bf16),
            pltpu.SemaphoreType.DMA((count,)),
            pltpu.SemaphoreType.DMA((count,)),
            pltpu.SemaphoreType.DMA((count,)),
            pltpu.SemaphoreType.DMA((count,)),
        ],
        compiler_params=pltpu.CompilerParams(vmem_limit_bytes=vmem_bytes),
        cost_estimate=estimate(20, rows * count),
        name="query_pull",
    )(*slots, *own, *other, *sums, wa, wb, ga, gb)
    return outs[0], outs[1], outs[2], outs[3:]


def key_kernel(count, n_sums, n_kept, entries, first, *refs):
    slots, refs = refs[:count], refs[count:]
    sums, refs = refs[:n_sums], refs[n_sums:]
    dots, refs = refs[:n_sums], refs[n_sums:]
    gain_ref, wa_ref, wb_ref, ga_ref, gb_ref, da_ref, db_ref = refs[:7]
    refs = refs[7:]
    kept, refs = refs[:n_kept], refs[n_kept:]
    out, refs = refs[:count], refs[count:]
    held, dah, dal, dbh, dbl, out_held, sem_k, sem_o = refs[:8]
    kept_held, kept_sems = refs[8 : 8 + n_kept], refs[8 + n_kept :]
    width = wb_ref.shape[0]
    fetch_all(slots, held, sem_k)
    for source, target, sems in zip(kept, kept_held, kept_sems):
        for j in range(count):
            pltpu.make_async_copy(source.at[first + j], target.at[j], sems.at[j]).start()
    gain = gain_ref[0]
    rms, scale = scale_of(sums, entries)
    product = dots[0][0:1, 0:1]
    for more in dots[1:]:
        product = product + more[0:1, 0:1]
    pull = product / (scale * scale * entries * rms)
    for d_ref, g_ref, h_ref, l_ref in (
        (da_ref, ga_ref, dah, dal),
        (db_ref, gb_ref, dbh, dbl),
    ):
        h_ref[...], l_ref[...] = halves(
            (d_ref[...] * (1.0 / scale) - g_ref[...] * pull) * (-inner_rate)
        )

    @pl.loop(0, count)
    def _(j):
        pltpu.make_async_copy(slots[0], held.at[j], sem_k.at[j]).wait()
        for source, target, sems in zip(kept, kept_held, kept_sems):
            pltpu.make_async_copy(source.at[first], target.at[j], sems.at[j]).wait()
        keys = held[j, :, :width]
        mixed = nn(keys, wa_ref[...]) * gain
        moved = two_right(nn, keys, (dah[...], dal[...])) * gain
        u, w = mixed[:, :width], mixed[:, width:]
        du, dw = moved[:, :width], moved[:, width:]
        sg = sigmoid(u)
        act = u * sg
        rest = 1.0 - sg
        slope = sg * (1.0 + u * rest)
        bend = sg * rest * (2.0 + u * (rest - sg))
        db = (dbh[...], dbl[...])
        hidden = halves(act * w)
        shift = two(nn, halves(slope * du * w + act * dw), wb_ref[...]) + three(nn, hidden, db)
        out_held[j, :, width:] = (-shift).astype(bf16)
        if n_kept:
            e2, hb = halves(kept_held[0][j]), kept_held[1][j]
        else:
            values = held[j, :, width : 2 * width].astype(f32)
            e2 = halves(two(nn, hidden, wb_ref[...]) - values)
            hb = two(nt, e2, wb_ref[...])
        back = two(nt, halves(shift), wb_ref[...]) + three(nt, e2, db)
        ub = halves(back * w * slope + hb * (bend * du * w + slope * dw))
        wbar = halves(back * act + hb * slope * du)
        ut = halves(hb * slope * w)
        wt = halves(hb * act)
        grad = (
            two(nt, ub, wa_ref[:, :width])
            + two(nt, wbar, wa_ref[:, width:])
            + three(nt, ut, (dah[:, :width], dal[:, :width]))
            + three(nt, wt, (dah[:, width:], dal[:, width:]))
        )
        out_held[j, :, :width] = (grad * gain).astype(bf16)

    copies = [pltpu.make_async_copy(out_held.at[j], out[j], sem_o.at[j]) for j in range(count)]
    for copy in copies:
        copy.start()
    for copy in copies:
        copy.wait()


def call_key(slots, sums, dots, entries, first, gain, wa, wb, ga, gb, da, db, *kept):
    count = len(slots)
    rows, width = slots[0].shape[0], wb.shape[0]
    return pl.pallas_call(
        partial(key_kernel, count, len(sums), len(kept), entries, first),
        out_shape=(shape_of(rows, 2 * width, dtype=bf16),) * count,
        in_specs=[any_spec()] * count
        + [vmem_spec()] * (2 * len(sums))
        + [smem_spec()]
        + [vmem_spec()] * 6
        + [any_spec()] * len(kept),
        out_specs=[any_spec()] * count,
        scratch_shapes=[
            pltpu.VMEM((count,) + slots[0].shape, bf16),
            pltpu.VMEM((width, 2 * width), bf16),
            pltpu.VMEM((width, 2 * width), bf16),
            pltpu.VMEM((width, width), bf16),
            pltpu.VMEM((width, width), bf16),
            pltpu.VMEM((count, rows, 2 * width), bf16),
            pltpu.SemaphoreType.DMA((count,)),
            pltpu.SemaphoreType.DMA((count,)),
        ]
        + [pltpu.VMEM((count, rows, width), f32)] * len(kept)
        + [pltpu.SemaphoreType.DMA((count,))] * len(kept),
        compiler_params=pltpu.CompilerParams(vmem_limit_bytes=vmem_bytes),
        cost_estimate=estimate(26, rows * count),
        name="key_pull",
    )(*slots, *sums, *dots, gain, wa, wb, ga, gb, da, db, *kept)


def per_device(queries, keys, values, fast_in, fast_out, key_gain, out_proj, grad_out):
    toks, heads = lax.axis_size("tok"), lax.axis_size("head")
    low, high = toks // 2 - 1, toks // 2
    width = fast_out.shape[1]
    entries = float(heads * (fast_in.shape[1] * fast_in.shape[2] + width * fast_out.shape[2]))
    wa, wb = fast_in[0], fast_out[0]
    place, head = lax.axis_index("tok"), lax.axis_index("head")
    core = lax.rem(head, 2)
    line = sorted(range(toks), key=lambda t: (abs(t - low), t))
    mirror = [toks - 1 - t for t in line]
    swap = tuple(mirror.index(t) for t in line)

    def root(h):
        return high if h % 2 else low

    def flat(t, h):
        return t * heads + h

    both = ("tok", "head")

    def to_root(j):
        return [(flat((mirror if h % 2 else line)[j], h), flat(root(h), h)) for h in range(heads)]

    def from_root(j):
        return [(b, a) for a, b in to_root(j)]

    rows_in = jnp.concatenate([keys, values, queries], axis=1)
    slots = [rows_in] + [lax.ppermute(rows_in, both, to_root(j)) for j in range(1, toks)]

    ga, gb, squares, *kept = call_inner_grad(slots, toks <= 8, key_gain, wa, wb)

    def exchange(value):
        across = [
            (flat(root(h), h), flat(root(h ^ 1), h ^ 1)) for h in range(heads)
        ]
        value = value + lax.ppermute(value, both, across)
        step = 2
        while step < heads:
            far = [(flat(root(h), h), flat(root(h), h ^ step)) for h in range(heads)]
            more = lax.ppermute(value, both, far)
            step *= 2
            if step < heads:
                value = value + more
            else:
                return value, more
        return (value,)

    sums = exchange(squares)

    blocks = [out_proj] + [
        lax.ppermute(out_proj, "tok", [(low - j, low), (high + j, high)])
        for j in range(1, toks // 2)
    ]
    quarter = grad_out.shape[1] // 4

    def side_of(parts):
        if len(parts) == 1:
            return parts[0]
        return jnp.where(
            place <= low, jnp.concatenate(parts[::-1], axis=1), jnp.concatenate(parts, axis=1)
        )

    near, far = side_of(blocks[: toks // 4]), side_of(blocks[toks // 4 :])
    w_mine = jnp.where(core == 0, near, far)
    w_theirs = jnp.where(core == 0, far, near)

    def columns(which, half_is_low):
        index = jnp.where(half_is_low, 1 - which, 2 + which)
        return lax.dynamic_slice_in_dim(grad_out, index * quarter, quarter, axis=1)

    def product(mine, theirs):
        return (
            lax.dot_general(mine, w_mine, (((1,), (1,)), ((), ())), preferred_element_type=f32)
            + lax.dot_general(
                theirs, w_theirs, (((1,), (1,)), ((), ())), preferred_element_type=f32
            )
        )

    cores = [(h, h ^ 1) for h in range(heads)]
    at_low = place <= low
    partials = [product(columns(core, at_low), columns(1 - core, at_low))]
    for j in range(1, toks):
        piece = lax.ppermute(
            columns(core, place == line[j]), "tok", [(line[j], low), (mirror[j], high)]
        )
        partials.append(product(piece, lax.ppermute(piece, "head", cores)))
    over = [
        (flat(high, h), flat(low, h)) if h % 2 == 0 else (flat(low, h), flat(high, h))
        for h in range(heads)
    ]
    others = [lax.ppermute(partial_sum, both, over) for partial_sum in partials]

    da, db, dots, dq = call_query(
        slots, partials, others, swap, sums, entries, wa, wb, ga, gb
    )
    dots = exchange(dots)
    is_root = place == jnp.where(core == 0, low, high)

    def home(slot_outs):
        back = None
        for j in range(1, toks):
            got = lax.ppermute(slot_outs[j], both, from_root(j))
            back = got if back is None else back + got
        return jnp.where(is_root, slot_outs[0], back)

    d_queries = home(dq)
    first = toks // 2
    outs_far = call_key(
        slots[first:], sums, dots, entries, first, key_gain, wa, wb, ga, gb, da, db, *kept
    )
    outs_near = call_key(
        slots[:first], sums, dots, entries, 0, key_gain, wa, wb, ga, gb, da, db, *kept
    )
    pair = home(list(outs_near) + list(outs_far))
    return d_queries, pair[:, :width], pair[:, width:]


def solution(mesh):
    rows = P(("groups", "tok"), "head")
    return jax.shard_map(
        per_device,
        mesh=mesh,
        in_specs=(
            rows,
            rows,
            rows,
            P("head", None, None),
            P("head", None, None),
            P("head"),
            P("head", "tok"),
            P(("groups", "tok"), None),
        ),
        out_specs=(rows, rows, rows),
        check_vma=False,
    )
```

```python
from functools import partial

import jax
import jax.numpy as jnp
from jax import lax
from jax.experimental import pallas as pl
from jax.experimental.pallas import tpu as pltpu
from jax.sharding import PartitionSpec as P

f32 = jnp.float32
bf16 = jnp.bfloat16
inner_rate = 0.02
norm_eps = 1e-06
vmem_bytes = 56 * 1024 * 1024
MIB = 1024 * 1024
JOIN = 1


def halves(x):
    top = x.astype(bf16)
    return top, (x - top.astype(f32)).astype(bf16)


def nn(a, b):
    return lax.dot_general(a, b, (((1,), (0,)), ((), ())), preferred_element_type=f32)


def nt(a, b):
    return lax.dot_general(a, b, (((1,), (1,)), ((), ())), preferred_element_type=f32)


def tn(a, b):
    return lax.dot_general(a, b, (((0,), (0,)), ((), ())), preferred_element_type=f32)


def joined(dot, a, b):
    left, right = {nn: (1, 0), nt: (1, 1), tn: (0, 0)}[dot]
    return dot(jnp.concatenate(a, axis=left), jnp.concatenate(b, axis=right))


def two(dot, a, b):
    return joined(dot, a, (b, b))


def two_right(dot, a, b):
    return joined(dot, (a, a), b)


def three(dot, a, b):
    return joined(dot, (a[0], a[0], a[1]), (b[0], b[1], b[0]))


def sigmoid(u):
    return 1.0 / (1.0 + jnp.exp(-u))


def part(j, rows):
    return pl.ds(pl.multiple_of(j * rows, rows), rows)


def fetch(sources, held, sems):
    rows = held.shape[0] // len(sources)
    for j, source in enumerate(sources):
        pltpu.make_async_copy(source, held.at[part(j, rows)], sems.at[j]).start()

    def wait(j):
        pltpu.make_async_copy(sources[0], held.at[part(j, rows)], sems.at[j]).wait()

    return wait


def joined_loop(count, rows, waits, body):
    join = JOIN
    while count % join:
        join -= 1

    @pl.loop(0, count // join)
    def _(i):
        for wait in waits:
            for k in range(join):
                wait(i * join + k)
        body(part(i, rows * join))


def inner_grad_kernel(count, keep, *refs):
    slots = refs[:count]
    gain_ref, wa_ref, wb_ref, ga_ref, gb_ref, sq_ref = refs[count : count + 6]
    held, sems = refs[-2:]
    wait = fetch(slots, held, sems)
    gain = gain_ref[0]
    width = wb_ref.shape[0]
    ga_ref[...] = jnp.zeros_like(ga_ref)
    gb_ref[...] = jnp.zeros_like(gb_ref)

    def body(j):
        keys = held[j, :width]
        values = held[j, width : 2 * width].astype(f32)
        mixed = nn(keys, wa_ref[...]) * gain
        u, w = mixed[:, :width], mixed[:, width:]
        sg = sigmoid(u)
        act = u * sg
        hidden = halves(act * w)
        e = two(nn, hidden, wb_ref[...]) - values
        e2 = halves(e)
        hb = two(nt, e2, wb_ref[...])
        if keep:
            e_ref, hb_ref = refs[count + 6 : count + 8]
            e_ref[j] = e
            hb_ref[j] = hb
        gb_ref[...] += three(tn, hidden, e2)
        slope = sg * (1.0 + u * (1.0 - sg))
        ga_ref[:, :width] += two_right(tn, keys, halves(hb * w * slope))
        ga_ref[:, width:] += two_right(tn, keys, halves(hb * act))

    joined_loop(count, slots[0].shape[0], [wait], body)
    ga = ga_ref[...] * gain
    ga_ref[...] = ga
    gb = gb_ref[...]
    sq_ref[...] = jnp.zeros_like(sq_ref) + (jnp.sum(ga * ga) + jnp.sum(gb * gb))


def vmem_spec():
    return pl.BlockSpec(memory_space=pltpu.VMEM)


def any_spec():
    return pl.BlockSpec(memory_space=pl.ANY)


def smem_spec():
    return pl.BlockSpec(memory_space=pltpu.SMEM)


def shape_of(*dims, dtype=f32):
    return jax.ShapeDtypeStruct(dims, dtype)


def estimate(units, rows):
    return pl.CostEstimate(
        flops=int(units * 2 * rows * 512 * 512), bytes_accessed=MIB, transcendentals=0
    )


def call_inner_grad(slots, keep, gain, wa, wb):
    count = len(slots)
    kept = 2 if keep else 0
    rows, width = slots[0].shape[0], wb.shape[0]
    return pl.pallas_call(
        partial(inner_grad_kernel, count, keep),
        out_shape=(shape_of(width, 2 * width), shape_of(width, width), shape_of(8, 128))
        + (shape_of(count * rows, width),) * kept,
        in_specs=[any_spec()] * count + [smem_spec(), vmem_spec(), vmem_spec()],
        out_specs=[vmem_spec()] * (3 + kept),
        scratch_shapes=[
            pltpu.VMEM((count * rows, slots[0].shape[1]), bf16),
            pltpu.SemaphoreType.DMA((count,)),
        ],
        compiler_params=pltpu.CompilerParams(vmem_limit_bytes=vmem_bytes),
        cost_estimate=estimate(13, rows * count),
        name="inner_grad",
    )(*slots, gain, wa, wb)


def scale_of(sums, entries):
    total = sums[0][0:1, 0:1]
    for more in sums[1:]:
        total = total + more[0:1, 0:1]
    rms = jnp.sqrt(total / entries)
    return rms, rms + norm_eps


def query_kernel(count, n_sums, entries, swap, *refs):
    slots, refs = refs[:count], refs[count:]
    own, refs = refs[:count], refs[count:]
    other, refs = refs[:count], refs[count:]
    sums, refs = refs[:n_sums], refs[n_sums:]
    (wa_ref, wb_ref, ga_ref, gb_ref), refs = refs[:4], refs[4:]
    (da_ref, db_ref, p_ref), refs = refs[:3], refs[3:]
    dq, refs = refs[:count], refs[count:]
    held, left, right, ah, al, bh, bl, dq_held, sem_q, sem_l, sem_r, sem_o = refs
    width = wb_ref.shape[0]
    waits = [
        fetch([slot.at[:, 2 * width : 3 * width] for slot in slots], held, sem_q),
        fetch(own, left, sem_l),
        fetch([other[swap[j]] for j in range(count)], right, sem_r),
    ]
    _, scale = scale_of(sums, entries)
    rate = inner_rate / scale
    ah[...], al[...] = halves(wa_ref[...].astype(f32) - ga_ref[...] * rate)
    bh[...], bl[...] = halves(wb_ref[...].astype(f32) - gb_ref[...] * rate)
    da_ref[...] = jnp.zeros_like(da_ref)
    db_ref[...] = jnp.zeros_like(db_ref)

    def body(j):
        queries = held[j]
        d_out = halves(left[j] + right[j])
        a = (ah[...], al[...])
        b = (bh[...], bl[...])
        mixed = two_right(nn, queries, a)
        u, w = mixed[:, :width], mixed[:, width:]
        sg = sigmoid(u)
        act = u * sg
        hb = three(nt, d_out, b)
        db_ref[...] += three(tn, halves(act * w), d_out)
        slope = sg * (1.0 + u * (1.0 - sg))
        ub = halves(hb * w * slope)
        wbar = halves(hb * act)
        da_ref[:, :width] += two_right(tn, queries, ub)
        da_ref[:, width:] += two_right(tn, queries, wbar)
        back = three(nt, ub, (ah[:, :width], al[:, :width])) + three(
            nt, wbar, (ah[:, width:], al[:, width:])
        )
        dq_held[j] = back.astype(bf16)

    rows = slots[0].shape[0]
    joined_loop(count, rows, waits, body)
    copies = [
        pltpu.make_async_copy(dq_held.at[part(j, rows)], dq[j], sem_o.at[j]) for j in range(count)
    ]
    for copy in copies:
        copy.start()
    total = jnp.sum(ga_ref[...] * da_ref[...]) + jnp.sum(gb_ref[...] * db_ref[...])
    p_ref[...] = jnp.zeros_like(p_ref) + total
    for copy in copies:
        copy.wait()


def call_query(slots, own, other, swap, sums, entries, wa, wb, ga, gb):
    count = len(slots)
    rows, width = slots[0].shape[0], wb.shape[0]
    outs = pl.pallas_call(
        partial(query_kernel, count, len(sums), entries, swap),
        out_shape=(shape_of(width, 2 * width), shape_of(width, width), shape_of(8, 128))
        + (shape_of(rows, width, dtype=bf16),) * count,
        in_specs=[any_spec()] * (3 * count) + [vmem_spec()] * (len(sums) + 4),
        out_specs=[vmem_spec()] * 3 + [any_spec()] * count,
        scratch_shapes=[
            pltpu.VMEM((count * rows, width), bf16),
            pltpu.VMEM((count * rows, width), f32),
            pltpu.VMEM((count * rows, width), f32),
            pltpu.VMEM((width, 2 * width), bf16),
            pltpu.VMEM((width, 2 * width), bf16),
            pltpu.VMEM((width, width), bf16),
            pltpu.VMEM((width, width), bf16),
            pltpu.VMEM((count * rows, width), bf16),
            pltpu.SemaphoreType.DMA((count,)),
            pltpu.SemaphoreType.DMA((count,)),
            pltpu.SemaphoreType.DMA((count,)),
            pltpu.SemaphoreType.DMA((count,)),
        ],
        compiler_params=pltpu.CompilerParams(vmem_limit_bytes=vmem_bytes),
        cost_estimate=estimate(20, rows * count),
        name="query_pull",
    )(*slots, *own, *other, *sums, wa, wb, ga, gb)
    return outs[0], outs[1], outs[2], outs[3:]


def key_kernel(count, n_sums, n_kept, entries, first, *refs):
    slots, refs = refs[:count], refs[count:]
    sums, refs = refs[:n_sums], refs[n_sums:]
    dots, refs = refs[:n_sums], refs[n_sums:]
    gain_ref, wa_ref, wb_ref, ga_ref, gb_ref, da_ref, db_ref = refs[:7]
    refs = refs[7:]
    kept, refs = refs[:n_kept], refs[n_kept:]
    out, refs = refs[:count], refs[count:]
    held, dah, dal, dbh, dbl, out_held, sem_k, sem_o = refs[:8]
    kept_held, kept_sems = refs[8 : 8 + n_kept], refs[8 + n_kept :]
    width = wb_ref.shape[0]
    rows = slots[0].shape[0]
    waits = [fetch(slots, held, sem_k)]
    for source, target, sems in zip(kept, kept_held, kept_sems):
        waits.append(
            fetch([source.at[part(first + j, rows)] for j in range(count)], target, sems)
        )
    gain = gain_ref[0]
    rms, scale = scale_of(sums, entries)
    product = dots[0][0:1, 0:1]
    for more in dots[1:]:
        product = product + more[0:1, 0:1]
    pull = product / (scale * scale * entries * rms)
    for d_ref, g_ref, h_ref, l_ref in (
        (da_ref, ga_ref, dah, dal),
        (db_ref, gb_ref, dbh, dbl),
    ):
        h_ref[...], l_ref[...] = halves(
            (d_ref[...] * (1.0 / scale) - g_ref[...] * pull) * (-inner_rate)
        )

    def body(j):
        keys = held[j, :width]
        mixed = nn(keys, wa_ref[...]) * gain
        moved = two_right(nn, keys, (dah[...], dal[...])) * gain
        u, w = mixed[:, :width], mixed[:, width:]
        du, dw = moved[:, :width], moved[:, width:]
        sg = sigmoid(u)
        act = u * sg
        rest = 1.0 - sg
        slope = sg * (1.0 + u * rest)
        bend = sg * rest * (2.0 + u * (rest - sg))
        db = (dbh[...], dbl[...])
        hidden = halves(act * w)
        shift = two(nn, halves(slope * du * w + act * dw), wb_ref[...]) + three(nn, hidden, db)
        out_held[j, width:] = (-shift).astype(bf16)
        if n_kept:
            e2, hb = halves(kept_held[0][j]), kept_held[1][j]
        else:
            values = held[j, width : 2 * width].astype(f32)
            e2 = halves(two(nn, hidden, wb_ref[...]) - values)
            hb = two(nt, e2, wb_ref[...])
        back = two(nt, halves(shift), wb_ref[...]) + three(nt, e2, db)
        ub = halves(back * w * slope + hb * (bend * du * w + slope * dw))
        wbar = halves(back * act + hb * slope * du)
        ut = halves(hb * slope * w)
        wt = halves(hb * act)
        grad = (
            two(nt, ub, wa_ref[:, :width])
            + two(nt, wbar, wa_ref[:, width:])
            + three(nt, ut, (dah[:, :width], dal[:, :width]))
            + three(nt, wt, (dah[:, width:], dal[:, width:]))
        )
        out_held[j, :width] = (grad * gain).astype(bf16)

    joined_loop(count, rows, waits, body)
    copies = [
        pltpu.make_async_copy(out_held.at[part(j, rows)], out[j], sem_o.at[j]) for j in range(count)
    ]
    for copy in copies:
        copy.start()
    for copy in copies:
        copy.wait()


def call_key(slots, sums, dots, entries, first, gain, wa, wb, ga, gb, da, db, *kept):
    count = len(slots)
    rows, width = slots[0].shape[0], wb.shape[0]
    return pl.pallas_call(
        partial(key_kernel, count, len(sums), len(kept), entries, first),
        out_shape=(shape_of(rows, 2 * width, dtype=bf16),) * count,
        in_specs=[any_spec()] * count
        + [vmem_spec()] * (2 * len(sums))
        + [smem_spec()]
        + [vmem_spec()] * 6
        + [any_spec()] * len(kept),
        out_specs=[any_spec()] * count,
        scratch_shapes=[
            pltpu.VMEM((count * rows, slots[0].shape[1]), bf16),
            pltpu.VMEM((width, 2 * width), bf16),
            pltpu.VMEM((width, 2 * width), bf16),
            pltpu.VMEM((width, width), bf16),
            pltpu.VMEM((width, width), bf16),
            pltpu.VMEM((count * rows, 2 * width), bf16),
            pltpu.SemaphoreType.DMA((count,)),
            pltpu.SemaphoreType.DMA((count,)),
        ]
        + [pltpu.VMEM((count * rows, width), f32)] * len(kept)
        + [pltpu.SemaphoreType.DMA((count,))] * len(kept),
        compiler_params=pltpu.CompilerParams(vmem_limit_bytes=vmem_bytes),
        cost_estimate=estimate(26, rows * count),
        name="key_pull",
    )(*slots, *sums, *dots, gain, wa, wb, ga, gb, da, db, *kept)


def any_line(queries, keys, values, fast_in, fast_out, key_gain, out_proj, grad_out):
    toks, heads = lax.axis_size("tok"), lax.axis_size("head")
    low, high = toks // 2 - 1, toks // 2
    width = fast_out.shape[1]
    entries = float(heads * (fast_in.shape[1] * fast_in.shape[2] + width * fast_out.shape[2]))
    wa, wb = fast_in[0], fast_out[0]
    place, head = lax.axis_index("tok"), lax.axis_index("head")
    core = lax.rem(head, 2)
    line = sorted(range(toks), key=lambda t: (abs(t - low), t))
    mirror = [toks - 1 - t for t in line]
    swap = tuple(mirror.index(t) for t in line)

    def root(h):
        return high if h % 2 else low

    def flat(t, h):
        return t * heads + h

    both = ("tok", "head")

    def to_root(j):
        return [(flat((mirror if h % 2 else line)[j], h), flat(root(h), h)) for h in range(heads)]

    def from_root(j):
        return [(b, a) for a, b in to_root(j)]

    rows_in = jnp.concatenate([keys, values, queries], axis=1)
    slots = [rows_in] + [lax.ppermute(rows_in, both, to_root(j)) for j in range(1, toks)]

    ga, gb, squares, *kept = call_inner_grad(slots, toks <= 8, key_gain, wa, wb)

    def exchange(value):
        parts = [value]
        for step in range(1, heads):
            turn = [(h, (h + step) % heads) for h in range(heads)]
            parts.append(
                lax.ppermute(value, both, [(flat(root(a), a), flat(root(b), b)) for a, b in turn])
            )
        return parts

    sums = exchange(squares)

    blocks = [out_proj] + [
        lax.ppermute(out_proj, "tok", [(low - j, low), (high + j, high)])
        for j in range(1, toks // 2)
    ]
    quarter = grad_out.shape[1] // 4

    def side_of(parts):
        if len(parts) == 1:
            return parts[0]
        return jnp.where(
            place <= low, jnp.concatenate(parts[::-1], axis=1), jnp.concatenate(parts, axis=1)
        )

    near, far = side_of(blocks[: toks // 4]), side_of(blocks[toks // 4 :])
    w_mine = jnp.where(core == 0, near, far)
    w_theirs = jnp.where(core == 0, far, near)

    def columns(which, half_is_low):
        index = jnp.where(half_is_low, 1 - which, 2 + which)
        return lax.dynamic_slice_in_dim(grad_out, index * quarter, quarter, axis=1)

    def product(mine, theirs):
        return (
            lax.dot_general(mine, w_mine, (((1,), (1,)), ((), ())), preferred_element_type=f32)
            + lax.dot_general(
                theirs, w_theirs, (((1,), (1,)), ((), ())), preferred_element_type=f32
            )
        )

    cores = [(h, h ^ 1) for h in range(heads)]
    at_low = place <= low
    partials = [product(columns(core, at_low), columns(1 - core, at_low))]
    for j in range(1, toks):
        piece = lax.ppermute(
            columns(core, place == line[j]), "tok", [(line[j], low), (mirror[j], high)]
        )
        partials.append(product(piece, lax.ppermute(piece, "head", cores)))
    over = [
        (flat(high, h), flat(low, h)) if h % 2 == 0 else (flat(low, h), flat(high, h))
        for h in range(heads)
    ]
    others = [lax.ppermute(partial_sum, both, over) for partial_sum in partials]

    da, db, dots, dq = call_query(
        slots, partials, others, swap, sums, entries, wa, wb, ga, gb
    )
    dots = exchange(dots)
    is_root = place == jnp.where(core == 0, low, high)

    def home(slot_outs):
        back = None
        for j in range(1, toks):
            got = lax.ppermute(slot_outs[j], both, from_root(j))
            back = got if back is None else back + got
        return jnp.where(is_root, slot_outs[0], back)

    d_queries = home(dq)
    first = toks // 2
    outs_far = call_key(
        slots[first:], sums, dots, entries, first, key_gain, wa, wb, ga, gb, da, db, *kept
    )
    outs_near = call_key(
        slots[:first], sums, dots, entries, 0, key_gain, wa, wb, ga, gb, da, db, *kept
    )
    pair = home(list(outs_near) + list(outs_far))
    return d_queries, pair[:, :width], pair[:, width:]


def call(kernel, name, units, rows, out_shape, out_specs, operands, scratch):
    light = name == "gradient"
    return pl.pallas_call(
        kernel,
        out_shape=out_shape,
        in_specs=[spec for _, spec in operands],
        out_specs=out_specs,
        scratch_shapes=scratch,
        compiler_params=pltpu.CompilerParams(vmem_limit_bytes=vmem_bytes),
        cost_estimate=estimate(0.01 if light else units, rows),
        name=name,
    )(*(value for value, _ in operands))


def held_rows(count, rows, columns, dtype):
    return [pltpu.VMEM((count * rows, columns), dtype), pltpu.SemaphoreType.DMA((count,))]


def gradient_kernel(count, *refs):
    slots = refs[:count]
    gain_ref, wa_ref, wb_ref, g_ref, sq_ref, kept, held, sems, misfit, sem_m = refs[count:]
    wait = fetch(slots, held, sems)
    gain = gain_ref[0]
    width, rows = wb_ref.shape[0], slots[0].shape[0]
    g_ref[...] = jnp.zeros_like(g_ref)

    @pl.loop(0, count)
    def _(j):
        wait(j)
        here = part(j, rows)
        keys = held[here, :width]
        values = held[here, width : 2 * width].astype(f32)
        mixed = nn(keys, wa_ref[...]) * gain
        u, w = mixed[:, :width], mixed[:, width:]
        sg = sigmoid(u)
        act = u * sg
        hidden = halves(act * w)
        e = two(nn, hidden, wb_ref[...]) - values
        misfit[here, :width] = e
        e2 = halves(e)
        hb = two(nt, e2, wb_ref[...])
        misfit[here, width:] = hb
        pltpu.make_async_copy(misfit.at[here], kept.at[here], sem_m.at[j]).start()
        g_ref[:, 2 * width :] += three(tn, hidden, e2)
        slope = sg * (1.0 + u * (1.0 - sg))
        g_ref[:, :width] += two_right(tn, keys, halves(hb * w * slope))
        g_ref[:, width : 2 * width] += two_right(tn, keys, halves(hb * act))

    ga = g_ref[:, : 2 * width] * gain
    g_ref[:, : 2 * width] = ga
    gb = g_ref[:, 2 * width :]
    sq_ref[...] = jnp.zeros_like(sq_ref) + (jnp.sum(ga * ga) + jnp.sum(gb * gb))
    for j in range(count):
        here = part(j, rows)
        pltpu.make_async_copy(misfit.at[here], kept.at[here], sem_m.at[j]).wait()


def call_gradient(slots, gain, wa, wb):
    count, (rows, columns) = len(slots), slots[0].shape
    width = wb.shape[0]
    return call(
        partial(gradient_kernel, count),
        "gradient",
        13,
        rows * count,
        (shape_of(width, 3 * width), shape_of(8, 128), shape_of(count * rows, 2 * width)),
        [vmem_spec(), vmem_spec(), any_spec()],
        [(x, any_spec()) for x in slots]
        + [(gain, smem_spec()), (wa, vmem_spec()), (wb, vmem_spec())],
        held_rows(count, rows, columns, bf16) + held_rows(count, rows, 2 * width, f32),
    )


def pull_query_kernel(opening, entries, *refs):
    slots, own, other = refs[:2], refs[2:4], refs[4:6]
    if opening:
        g_all, sum0, sum1, wa_ref, wb_ref, acc_ref, uh, ul, dq0, dq1 = refs[6:16]
    else:
        g_all, old, uh, ul, acc_ref, p_ref, mh, ml = refs[6:14]
    held, sem_q, left, sem_l, right, sem_r, g_ref, sem_g, sem_a = refs[-9:]
    width, rows = held.shape[1], slots[0].shape[0]
    both_in, gate, up, down = (
        slice(0, 2 * width),
        slice(0, width),
        slice(width, 2 * width),
        slice(2 * width, 3 * width),
    )
    waits = [
        fetch([block.at[:, down] for block in slots], held, sem_q),
        fetch(own, left, sem_l),
        fetch(other, right, sem_r),
    ]
    g_wait = fetch([g_all], g_ref, sem_g)
    if opening:
        g_wait(0)
        _, scale = scale_of((sum0, sum1), entries)
        rate = inner_rate / scale
        for w_ref, place in ((wa_ref, both_in), (wb_ref, down)):
            uh[:, place], ul[:, place] = halves(w_ref[...].astype(f32) - g_ref[:, place] * rate)
        acc_ref[...] = jnp.zeros_like(acc_ref)
    else:
        a_wait = fetch([old], acc_ref, sem_a)

    @pl.loop(0, 2)
    def _(j):
        for wait in waits:
            wait(j)
        here = part(j, rows)
        queries = held[here]
        d_out = halves(left[here] + right[here])
        mixed = two_right(nn, queries, (uh[:, both_in], ul[:, both_in]))
        u, w = mixed[:, :width], mixed[:, width:]
        sg = sigmoid(u)
        act = u * sg
        hb = three(nt, d_out, (uh[:, down], ul[:, down]))
        if not opening:

            @pl.when(j == 0)
            def _():
                a_wait(0)

        acc_ref[:, down] += three(tn, halves(act * w), d_out)
        slope = sg * (1.0 + u * (1.0 - sg))
        ub = halves(hb * w * slope)
        wbar = halves(hb * act)
        acc_ref[:, gate] += two_right(tn, queries, ub)
        acc_ref[:, up] += two_right(tn, queries, wbar)
        if not opening:
            for m_ref, gate_part, up_part in ((mh, ub[0], wbar[0]), (ml, ub[1], wbar[1])):
                m_ref[here, :width] = gate_part
                m_ref[here, width:] = up_part
            return
        back = three(nt, ub, (uh[:, gate], ul[:, gate])) + three(
            nt, wbar, (uh[:, up], ul[:, up])
        )
        for k, dq_ref in enumerate((dq0, dq1)):

            @pl.when(j == k)
            def _():
                dq_ref[...] = back.astype(bf16)

    if not opening:
        g_wait(0)
        p_ref[...] = jnp.zeros_like(p_ref) + jnp.sum(g_ref[...] * acc_ref[...])


def query_grad_kernel(mh, ml, uh, ul, *dqs):
    width = uh.shape[0]
    rows = mh.shape[0] // 2
    both_in = slice(0, 2 * width)
    for k, dq_ref in enumerate(dqs):
        here = slice(k * rows, (k + 1) * rows)
        back = three(nt, (mh[here], ml[here]), (uh[:, both_in], ul[:, both_in]))
        dq_ref[...] = back.astype(bf16)


def call_query_grad(mh, ml, uh, ul):
    rows, width = mh.shape[0] // 2, uh.shape[0]
    return call(
        query_grad_kernel,
        "query_grad",
        6,
        2 * rows,
        (shape_of(rows, width, dtype=bf16),) * 2,
        [vmem_spec()] * 2,
        [(x, vmem_spec()) for x in (mh, ml, uh, ul)],
        [],
    )


def call_pull_query(entries, slots, own, other, streams, more, opening):
    rows, width = slots[0].shape[0], slots[0].shape[1] // 3
    whole = shape_of(width, 3 * width)
    half = shape_of(width, 3 * width, dtype=bf16)
    dq = shape_of(rows, width, dtype=bf16)
    mixed = shape_of(2 * rows, 2 * width, dtype=bf16)
    outs = (whole, half, half, dq, dq) if opening else (whole, shape_of(8, 128), mixed, mixed)
    return call(
        partial(pull_query_kernel, opening, entries),
        "query_pull",
        20,
        rows * 2,
        outs,
        [vmem_spec()] * len(outs),
        [(x, any_spec()) for x in (*slots, *own, *other, *streams)]
        + [(x, vmem_spec()) for x in more],
        held_rows(2, rows, width, bf16)
        + held_rows(2, rows, width, f32)
        + held_rows(2, rows, width, f32)
        + held_rows(1, width, 3 * width, f32)
        + [pltpu.SemaphoreType.DMA((1,))],
    )


def pull_key_kernel(entries, blocks, *refs):
    count = len(blocks)
    slots, refs = refs[:count], refs[count:]
    kept, gain_ref, wa_ref, wb_ref = refs[:4]
    sum0, sum1, dot0, dot1, g_ref, du_ref = refs[4:10]
    out, scratch = refs[10 : 10 + count], refs[10 + count :]
    held, sem_k, kept_held, sem_e, dh, dl = scratch
    width, rows = wb_ref.shape[0], slots[0].shape[0]
    waits = [
        fetch(slots, held, sem_k),
        fetch([kept.at[part(block, rows)] for block in blocks], kept_held, sem_e),
    ]
    gain = gain_ref[0]
    rms, scale = scale_of((sum0, sum1), entries)
    pull = (dot0[0:1, 0:1] + dot1[0:1, 0:1]) / (scale * scale * entries * rms)
    dh[...], dl[...] = halves((du_ref[...] * (1.0 / scale) - g_ref[...] * pull) * (-inner_rate))
    both_in, gate, up, down = (
        slice(0, 2 * width),
        slice(0, width),
        slice(width, 2 * width),
        slice(2 * width, 3 * width),
    )

    @pl.loop(0, count)
    def _(j):
        for wait in waits:
            wait(j)
        here = part(j, rows)
        keys = held[here, :width]
        mixed = nn(keys, wa_ref[...]) * gain
        moved = two_right(nn, keys, (dh[:, both_in], dl[:, both_in])) * gain
        u, w = mixed[:, :width], mixed[:, width:]
        du, dw = moved[:, :width], moved[:, width:]
        sg = sigmoid(u)
        act = u * sg
        rest = 1.0 - sg
        slope = sg * (1.0 + u * rest)
        bend = sg * rest * (2.0 + u * (rest - sg))
        db = (dh[:, down], dl[:, down])
        shift = two(nn, halves(slope * du * w + act * dw), wb_ref[...]) + three(
            nn, halves(act * w), db
        )
        back = two(nt, halves(shift), wb_ref[...]) + three(
            nt, halves(kept_held[here, :width]), db
        )
        hb = kept_held[here, width:]
        ub = halves(back * w * slope + hb * (bend * du * w + slope * dw))
        wbar = halves(back * act + hb * slope * du)
        ut = halves(hb * slope * w)
        wt = halves(hb * act)
        grad = (
            two(nt, ub, wa_ref[:, :width])
            + two(nt, wbar, wa_ref[:, width:])
            + three(nt, ut, (dh[:, gate], dl[:, gate]))
            + three(nt, wt, (dh[:, up], dl[:, up]))
        )
        for k, out_ref in enumerate(out):

            @pl.when(j == k)
            def _():
                out_ref[:, :width] = (grad * gain).astype(bf16)
                out_ref[:, width:] = (-shift).astype(bf16)


def call_pull_key(blocks, entries, slots, kept, gain, wa, wb, terms):
    count, (rows, columns) = len(blocks), slots[0].shape
    width = wb.shape[0]
    return call(
        partial(pull_key_kernel, entries, blocks),
        "key_pull",
        26,
        rows * count,
        (shape_of(rows, 2 * width, dtype=bf16),) * count,
        [vmem_spec()] * count,
        [(slots[block], any_spec()) for block in blocks]
        + [(kept, any_spec()), (gain, smem_spec()), (wa, vmem_spec()), (wb, vmem_spec())]
        + [(x, vmem_spec()) for x in terms],
        held_rows(count, rows, columns, bf16)
        + held_rows(count, rows, 2 * width, f32)
        + [pltpu.VMEM((width, 3 * width), bf16)] * 2,
    )


def four_line(queries, keys, values, fast_in, fast_out, key_gain, out_proj, grad_out):
    toks, heads = 4, lax.axis_size("head")
    low, high = 1, 2
    width = fast_out.shape[1]
    entries = float(heads * (fast_in.shape[1] * fast_in.shape[2] + width * fast_out.shape[2]))
    place, head = lax.axis_index("tok"), lax.axis_index("head")
    core = lax.rem(head, 2)
    line, mirror = (1, 0, 2, 3), (2, 3, 1, 0)
    both = ("tok", "head")
    tie = lax.optimization_barrier

    def flat(t, h):
        return t * heads + h

    def root(h):
        return high if h % 2 else low

    def order(h):
        return mirror if h % 2 else line

    def to_root(j):
        return [(flat(order(h)[j], h), flat(root(h), h)) for h in range(heads)]

    def home(value, j):
        return lax.ppermute(value, both, [(b, a) for a, b in to_root(j)])

    is_root = place == jnp.where(core == 0, low, high)
    wa, wb = fast_in[0], fast_out[0]
    rows_in = jnp.concatenate([keys, values, queries], axis=1)
    slots = [rows_in] + [lax.ppermute(rows_in, both, to_root(j)) for j in range(1, toks)]

    far = lax.ppermute(out_proj, "tok", [(0, low), (3, high)])
    quarter = grad_out.shape[1] // 4

    def columns(array, which, half_is_low):
        index = jnp.where(half_is_low, 1 - which, 2 + which)
        return lax.dynamic_slice_in_dim(array, index * quarter, quarter, axis=1)

    def piece(array, j):
        return lax.ppermute(
            columns(array, core, place == line[j]), "tok", [(line[j], low), (mirror[j], high)]
        )

    def swap_cores(value):
        return lax.ppermute(value, "head", [(h, h ^ 1) for h in range(heads)])

    piece2 = piece(grad_out, 2)
    later, far, piece2, *slots = tie((grad_out, far, piece2, *slots))

    def exchange(value, pairs, step_pairs, beside=None):
        more = lax.ppermute(value, both, pairs)
        if beside is not None:
            outs, more = tie((beside(), more))
        value = value + more
        step = 2
        while True:
            more = lax.ppermute(value, both, step_pairs(step))
            step *= 2
            if step >= heads:
                return (value, more) if beside is None else (value, more, outs)
            value = value + more

    over = [
        (flat(high, h), flat(low, h)) if h % 2 == 0 else (flat(low, h), flat(high, h))
        for h in range(heads)
    ]
    root_pairs = [(flat(root(h), h), flat(root(h ^ 1), h ^ 1)) for h in range(heads)]

    def root_steps(step):
        return [(flat(root(h), h), flat(root(h), h ^ step)) for h in range(heads)]

    at_low = place <= low
    piece3 = piece(later, 3)
    piece1 = piece(later, 1)
    g, squares, kept = call_gradient(slots, key_gain, wa, wb)
    g, squares, far, piece2, mine0, theirs0 = tie(
        (
            g,
            squares,
            far,
            piece2,
            columns(later, core, at_low),
            columns(later, 1 - core, at_low),
        )
    )

    w_mine = jnp.where(core == 0, out_proj, far)
    w_theirs = jnp.where(core == 0, far, out_proj)

    def product(mine, theirs):
        return nt(mine, w_mine) + nt(theirs, w_theirs)

    own0 = product(mine0, theirs0)
    other2 = lax.ppermute(own0, both, over)
    own2 = product(piece2, swap_cores(piece2))
    other0 = lax.ppermute(own2, both, over)
    squares_in, *_ = tie((squares, own0, own2))
    sums = exchange(squares_in, root_pairs, root_steps)
    piece3, piece1, other0, other2, *sums = tie((piece3, piece1, other0, other2, *sums))

    own3 = product(piece3, swap_cores(piece3))
    other1 = lax.ppermute(own3, both, over)
    own1 = product(piece1, swap_cores(piece1))
    other3 = lax.ppermute(own1, both, over)
    own3, own1, *sums = tie((own3, own1, *sums))
    acc, uh, ul, dq0, dq2 = call_pull_query(
        entries, slots[0::2], (own0, own2), (other0, other2), (g,), (*sums, wa, wb), True
    )
    other1, other3, acc, uh, ul, dq2 = tie((other1, other3, acc, uh, ul, dq2))

    du, dots, mh, ml = call_pull_query(
        entries, slots[1::2], (own1, own3), (other1, other3), (g, acc), (uh, ul), False
    )
    du, dots, mh, ml = tie((du, dots, mh, ml))

    *dots, (dq1, dq3) = exchange(
        dots, root_pairs, root_steps, lambda: call_query_grad(mh, ml, uh, ul)
    )
    du, dq1, dq3, *dots = tie((du, dq1, dq3, *dots))

    terms = (*sums, *dots, g, du)
    dq1, dq2, dq3 = home(dq1, 1), home(dq2, 2), home(dq3, 3)
    out3, out2 = call_pull_key((3, 2), entries, slots, kept, key_gain, wa, wb, terms)
    out3, out2, dq1, dq2, dq3, *terms = tie((out3, out2, dq1, dq2, dq3, *terms))

    out3, out2 = home(out3, 3), home(out2, 2)
    out1, out0 = call_pull_key((1, 0), entries, slots, kept, key_gain, wa, wb, terms)
    d_queries = jnp.where(is_root, dq0, dq1 + dq2 + dq3)
    out3, out2, out1, out0, d_queries = tie((out3, out2, out1, out0, d_queries))

    pair = jnp.where(is_root, out0, home(out1, 1) + out2 + out3)
    return d_queries, pair[:, :width], pair[:, width:]


def per_device(*arrays):
    fits = lax.axis_size("tok") == 4 and lax.axis_size("head") >= 4
    return (four_line if fits else any_line)(*arrays)


def solution(mesh):
    rows = P(("groups", "tok"), "head")
    return jax.shard_map(
        per_device,
        mesh=mesh,
        in_specs=(
            rows,
            rows,
            rows,
            P("head", None, None),
            P("head", None, None),
            P("head"),
            P("head", "tok"),
            P(("groups", "tok"), None),
        ),
        out_specs=(rows, rows, rows),
        check_vma=False,
    )
```

```python
from functools import partial

import jax
import jax.numpy as jnp
from jax import lax
from jax.experimental import pallas as pl
from jax.experimental.pallas import tpu as pltpu
from jax.sharding import PartitionSpec as P

f32 = jnp.float32
bf16 = jnp.bfloat16
inner_rate = 0.02
norm_eps = 1e-06
vmem_bytes = 56 * 1024 * 1024
MIB = 1024 * 1024
JOIN = 1


def halves(x):
    top = x.astype(bf16)
    return top, (x - top.astype(f32)).astype(bf16)


def nn(a, b):
    return lax.dot_general(a, b, (((1,), (0,)), ((), ())), preferred_element_type=f32)


def nt(a, b):
    return lax.dot_general(a, b, (((1,), (1,)), ((), ())), preferred_element_type=f32)


def tn(a, b):
    return lax.dot_general(a, b, (((0,), (0,)), ((), ())), preferred_element_type=f32)


def joined(dot, a, b):
    left, right = {nn: (1, 0), nt: (1, 1), tn: (0, 0)}[dot]
    return dot(jnp.concatenate(a, axis=left), jnp.concatenate(b, axis=right))


def two(dot, a, b):
    return joined(dot, a, (b, b))


def two_right(dot, a, b):
    return joined(dot, (a, a), b)


def three(dot, a, b):
    return joined(dot, (a[0], a[0], a[1]), (b[0], b[1], b[0]))


def sigmoid(u):
    return 1.0 / (1.0 + jnp.exp(-u))


def part(j, rows):
    return pl.ds(pl.multiple_of(j * rows, rows), rows)


def fetch(sources, held, sems):
    rows = held.shape[0] // len(sources)
    for j, source in enumerate(sources):
        pltpu.make_async_copy(source, held.at[part(j, rows)], sems.at[j]).start()

    def wait(j):
        pltpu.make_async_copy(sources[0], held.at[part(j, rows)], sems.at[j]).wait()

    return wait


def joined_loop(count, rows, waits, body):
    join = JOIN
    while count % join:
        join -= 1

    @pl.loop(0, count // join)
    def _(i):
        for wait in waits:
            for k in range(join):
                wait(i * join + k)
        body(part(i, rows * join))


def inner_grad_kernel(count, keep, *refs):
    slots = refs[:count]
    gain_ref, wa_ref, wb_ref, ga_ref, gb_ref, sq_ref = refs[count : count + 6]
    held, sems = refs[-2:]
    wait = fetch(slots, held, sems)
    gain = gain_ref[0]
    width = wb_ref.shape[0]
    ga_ref[...] = jnp.zeros_like(ga_ref)
    gb_ref[...] = jnp.zeros_like(gb_ref)

    def body(j):
        keys = held[j, :width]
        values = held[j, width : 2 * width].astype(f32)
        mixed = nn(keys, wa_ref[...]) * gain
        u, w = mixed[:, :width], mixed[:, width:]
        sg = sigmoid(u)
        act = u * sg
        hidden = halves(act * w)
        e = two(nn, hidden, wb_ref[...]) - values
        e2 = halves(e)
        hb = two(nt, e2, wb_ref[...])
        if keep:
            e_ref, hb_ref = refs[count + 6 : count + 8]
            e_ref[j] = e
            hb_ref[j] = hb
        gb_ref[...] += three(tn, hidden, e2)
        slope = sg * (1.0 + u * (1.0 - sg))
        ga_ref[:, :width] += two_right(tn, keys, halves(hb * w * slope))
        ga_ref[:, width:] += two_right(tn, keys, halves(hb * act))

    joined_loop(count, slots[0].shape[0], [wait], body)
    ga = ga_ref[...] * gain
    ga_ref[...] = ga
    gb = gb_ref[...]
    sq_ref[...] = jnp.zeros_like(sq_ref) + (jnp.sum(ga * ga) + jnp.sum(gb * gb))


def vmem_spec():
    return pl.BlockSpec(memory_space=pltpu.VMEM)


def any_spec():
    return pl.BlockSpec(memory_space=pl.ANY)


def smem_spec():
    return pl.BlockSpec(memory_space=pltpu.SMEM)


def shape_of(*dims, dtype=f32):
    return jax.ShapeDtypeStruct(dims, dtype)


def estimate(units, rows):
    return pl.CostEstimate(
        flops=int(units * 2 * rows * 512 * 512), bytes_accessed=MIB, transcendentals=0
    )


def call_inner_grad(slots, keep, gain, wa, wb):
    count = len(slots)
    kept = 2 if keep else 0
    rows, width = slots[0].shape[0], wb.shape[0]
    return pl.pallas_call(
        partial(inner_grad_kernel, count, keep),
        out_shape=(shape_of(width, 2 * width), shape_of(width, width), shape_of(8, 128))
        + (shape_of(count * rows, width),) * kept,
        in_specs=[any_spec()] * count + [smem_spec(), vmem_spec(), vmem_spec()],
        out_specs=[vmem_spec()] * (3 + kept),
        scratch_shapes=[
            pltpu.VMEM((count * rows, slots[0].shape[1]), bf16),
            pltpu.SemaphoreType.DMA((count,)),
        ],
        compiler_params=pltpu.CompilerParams(vmem_limit_bytes=vmem_bytes),
        cost_estimate=estimate(13, rows * count),
        name="inner_grad",
    )(*slots, gain, wa, wb)


def scale_of(sums, entries):
    total = sums[0][0:1, 0:1]
    for more in sums[1:]:
        total = total + more[0:1, 0:1]
    rms = jnp.sqrt(total / entries)
    return rms, rms + norm_eps


def query_kernel(count, n_sums, entries, swap, *refs):
    slots, refs = refs[:count], refs[count:]
    own, refs = refs[:count], refs[count:]
    other, refs = refs[:count], refs[count:]
    sums, refs = refs[:n_sums], refs[n_sums:]
    (wa_ref, wb_ref, ga_ref, gb_ref), refs = refs[:4], refs[4:]
    (da_ref, db_ref, p_ref), refs = refs[:3], refs[3:]
    dq, refs = refs[:count], refs[count:]
    held, left, right, ah, al, bh, bl, dq_held, sem_q, sem_l, sem_r, sem_o = refs
    width = wb_ref.shape[0]
    waits = [
        fetch([slot.at[:, 2 * width : 3 * width] for slot in slots], held, sem_q),
        fetch(own, left, sem_l),
        fetch([other[swap[j]] for j in range(count)], right, sem_r),
    ]
    _, scale = scale_of(sums, entries)
    rate = inner_rate / scale
    ah[...], al[...] = halves(wa_ref[...].astype(f32) - ga_ref[...] * rate)
    bh[...], bl[...] = halves(wb_ref[...].astype(f32) - gb_ref[...] * rate)
    da_ref[...] = jnp.zeros_like(da_ref)
    db_ref[...] = jnp.zeros_like(db_ref)

    def body(j):
        queries = held[j]
        d_out = halves(left[j] + right[j])
        a = (ah[...], al[...])
        b = (bh[...], bl[...])
        mixed = two_right(nn, queries, a)
        u, w = mixed[:, :width], mixed[:, width:]
        sg = sigmoid(u)
        act = u * sg
        hb = three(nt, d_out, b)
        db_ref[...] += three(tn, halves(act * w), d_out)
        slope = sg * (1.0 + u * (1.0 - sg))
        ub = halves(hb * w * slope)
        wbar = halves(hb * act)
        da_ref[:, :width] += two_right(tn, queries, ub)
        da_ref[:, width:] += two_right(tn, queries, wbar)
        back = three(nt, ub, (ah[:, :width], al[:, :width])) + three(
            nt, wbar, (ah[:, width:], al[:, width:])
        )
        dq_held[j] = back.astype(bf16)

    rows = slots[0].shape[0]
    joined_loop(count, rows, waits, body)
    copies = [
        pltpu.make_async_copy(dq_held.at[part(j, rows)], dq[j], sem_o.at[j]) for j in range(count)
    ]
    for copy in copies:
        copy.start()
    total = jnp.sum(ga_ref[...] * da_ref[...]) + jnp.sum(gb_ref[...] * db_ref[...])
    p_ref[...] = jnp.zeros_like(p_ref) + total
    for copy in copies:
        copy.wait()


def call_query(slots, own, other, swap, sums, entries, wa, wb, ga, gb):
    count = len(slots)
    rows, width = slots[0].shape[0], wb.shape[0]
    outs = pl.pallas_call(
        partial(query_kernel, count, len(sums), entries, swap),
        out_shape=(shape_of(width, 2 * width), shape_of(width, width), shape_of(8, 128))
        + (shape_of(rows, width, dtype=bf16),) * count,
        in_specs=[any_spec()] * (3 * count) + [vmem_spec()] * (len(sums) + 4),
        out_specs=[vmem_spec()] * 3 + [any_spec()] * count,
        scratch_shapes=[
            pltpu.VMEM((count * rows, width), bf16),
            pltpu.VMEM((count * rows, width), f32),
            pltpu.VMEM((count * rows, width), f32),
            pltpu.VMEM((width, 2 * width), bf16),
            pltpu.VMEM((width, 2 * width), bf16),
            pltpu.VMEM((width, width), bf16),
            pltpu.VMEM((width, width), bf16),
            pltpu.VMEM((count * rows, width), bf16),
            pltpu.SemaphoreType.DMA((count,)),
            pltpu.SemaphoreType.DMA((count,)),
            pltpu.SemaphoreType.DMA((count,)),
            pltpu.SemaphoreType.DMA((count,)),
        ],
        compiler_params=pltpu.CompilerParams(vmem_limit_bytes=vmem_bytes),
        cost_estimate=estimate(20, rows * count),
        name="query_pull",
    )(*slots, *own, *other, *sums, wa, wb, ga, gb)
    return outs[0], outs[1], outs[2], outs[3:]


def key_kernel(count, n_sums, n_kept, entries, first, *refs):
    slots, refs = refs[:count], refs[count:]
    sums, refs = refs[:n_sums], refs[n_sums:]
    dots, refs = refs[:n_sums], refs[n_sums:]
    gain_ref, wa_ref, wb_ref, ga_ref, gb_ref, da_ref, db_ref = refs[:7]
    refs = refs[7:]
    kept, refs = refs[:n_kept], refs[n_kept:]
    out, refs = refs[:count], refs[count:]
    held, dah, dal, dbh, dbl, out_held, sem_k, sem_o = refs[:8]
    kept_held, kept_sems = refs[8 : 8 + n_kept], refs[8 + n_kept :]
    width = wb_ref.shape[0]
    rows = slots[0].shape[0]
    waits = [fetch(slots, held, sem_k)]
    for source, target, sems in zip(kept, kept_held, kept_sems):
        waits.append(
            fetch([source.at[part(first + j, rows)] for j in range(count)], target, sems)
        )
    gain = gain_ref[0]
    rms, scale = scale_of(sums, entries)
    product = dots[0][0:1, 0:1]
    for more in dots[1:]:
        product = product + more[0:1, 0:1]
    pull = product / (scale * scale * entries * rms)
    for d_ref, g_ref, h_ref, l_ref in (
        (da_ref, ga_ref, dah, dal),
        (db_ref, gb_ref, dbh, dbl),
    ):
        h_ref[...], l_ref[...] = halves(
            (d_ref[...] * (1.0 / scale) - g_ref[...] * pull) * (-inner_rate)
        )

    def body(j):
        keys = held[j, :width]
        mixed = nn(keys, wa_ref[...]) * gain
        moved = two_right(nn, keys, (dah[...], dal[...])) * gain
        u, w = mixed[:, :width], mixed[:, width:]
        du, dw = moved[:, :width], moved[:, width:]
        sg = sigmoid(u)
        act = u * sg
        rest = 1.0 - sg
        slope = sg * (1.0 + u * rest)
        bend = sg * rest * (2.0 + u * (rest - sg))
        db = (dbh[...], dbl[...])
        hidden = halves(act * w)
        shift = two(nn, halves(slope * du * w + act * dw), wb_ref[...]) + three(nn, hidden, db)
        out_held[j, width:] = (-shift).astype(bf16)
        if n_kept:
            e2, hb = halves(kept_held[0][j]), kept_held[1][j]
        else:
            values = held[j, width : 2 * width].astype(f32)
            e2 = halves(two(nn, hidden, wb_ref[...]) - values)
            hb = two(nt, e2, wb_ref[...])
        back = two(nt, halves(shift), wb_ref[...]) + three(nt, e2, db)
        ub = halves(back * w * slope + hb * (bend * du * w + slope * dw))
        wbar = halves(back * act + hb * slope * du)
        ut = halves(hb * slope * w)
        wt = halves(hb * act)
        grad = (
            two(nt, ub, wa_ref[:, :width])
            + two(nt, wbar, wa_ref[:, width:])
            + three(nt, ut, (dah[:, :width], dal[:, :width]))
            + three(nt, wt, (dah[:, width:], dal[:, width:]))
        )
        out_held[j, :width] = (grad * gain).astype(bf16)

    joined_loop(count, rows, waits, body)
    copies = [
        pltpu.make_async_copy(out_held.at[part(j, rows)], out[j], sem_o.at[j]) for j in range(count)
    ]
    for copy in copies:
        copy.start()
    for copy in copies:
        copy.wait()


def call_key(slots, sums, dots, entries, first, gain, wa, wb, ga, gb, da, db, *kept):
    count = len(slots)
    rows, width = slots[0].shape[0], wb.shape[0]
    return pl.pallas_call(
        partial(key_kernel, count, len(sums), len(kept), entries, first),
        out_shape=(shape_of(rows, 2 * width, dtype=bf16),) * count,
        in_specs=[any_spec()] * count
        + [vmem_spec()] * (2 * len(sums))
        + [smem_spec()]
        + [vmem_spec()] * 6
        + [any_spec()] * len(kept),
        out_specs=[any_spec()] * count,
        scratch_shapes=[
            pltpu.VMEM((count * rows, slots[0].shape[1]), bf16),
            pltpu.VMEM((width, 2 * width), bf16),
            pltpu.VMEM((width, 2 * width), bf16),
            pltpu.VMEM((width, width), bf16),
            pltpu.VMEM((width, width), bf16),
            pltpu.VMEM((count * rows, 2 * width), bf16),
            pltpu.SemaphoreType.DMA((count,)),
            pltpu.SemaphoreType.DMA((count,)),
        ]
        + [pltpu.VMEM((count * rows, width), f32)] * len(kept)
        + [pltpu.SemaphoreType.DMA((count,))] * len(kept),
        compiler_params=pltpu.CompilerParams(vmem_limit_bytes=vmem_bytes),
        cost_estimate=estimate(26, rows * count),
        name="key_pull",
    )(*slots, *sums, *dots, gain, wa, wb, ga, gb, da, db, *kept)


def any_line(queries, keys, values, fast_in, fast_out, key_gain, out_proj, grad_out):
    toks, heads = lax.axis_size("tok"), lax.axis_size("head")
    low, high = toks // 2 - 1, toks // 2
    width = fast_out.shape[1]
    entries = float(heads * (fast_in.shape[1] * fast_in.shape[2] + width * fast_out.shape[2]))
    wa, wb = fast_in[0], fast_out[0]
    place, head = lax.axis_index("tok"), lax.axis_index("head")
    core = lax.rem(head, 2)
    line = sorted(range(toks), key=lambda t: (abs(t - low), t))
    mirror = [toks - 1 - t for t in line]
    swap = tuple(mirror.index(t) for t in line)

    def root(h):
        return high if h % 2 else low

    def flat(t, h):
        return t * heads + h

    both = ("tok", "head")

    def to_root(j):
        return [(flat((mirror if h % 2 else line)[j], h), flat(root(h), h)) for h in range(heads)]

    def from_root(j):
        return [(b, a) for a, b in to_root(j)]

    rows_in = jnp.concatenate([keys, values, queries], axis=1)
    slots = [rows_in] + [lax.ppermute(rows_in, both, to_root(j)) for j in range(1, toks)]

    ga, gb, squares, *kept = call_inner_grad(slots, toks <= 8, key_gain, wa, wb)

    def exchange(value):
        parts = [value]
        for step in range(1, heads):
            turn = [(h, (h + step) % heads) for h in range(heads)]
            parts.append(
                lax.ppermute(value, both, [(flat(root(a), a), flat(root(b), b)) for a, b in turn])
            )
        return parts

    sums = exchange(squares)

    blocks = [out_proj] + [
        lax.ppermute(out_proj, "tok", [(low - j, low), (high + j, high)])
        for j in range(1, toks // 2)
    ]
    quarter = grad_out.shape[1] // 4

    def side_of(parts):
        if len(parts) == 1:
            return parts[0]
        return jnp.where(
            place <= low, jnp.concatenate(parts[::-1], axis=1), jnp.concatenate(parts, axis=1)
        )

    near, far = side_of(blocks[: toks // 4]), side_of(blocks[toks // 4 :])
    w_mine = jnp.where(core == 0, near, far)
    w_theirs = jnp.where(core == 0, far, near)

    def columns(which, half_is_low):
        index = jnp.where(half_is_low, 1 - which, 2 + which)
        return lax.dynamic_slice_in_dim(grad_out, index * quarter, quarter, axis=1)

    def product(mine, theirs):
        return (
            lax.dot_general(mine, w_mine, (((1,), (1,)), ((), ())), preferred_element_type=f32)
            + lax.dot_general(
                theirs, w_theirs, (((1,), (1,)), ((), ())), preferred_element_type=f32
            )
        )

    cores = [(h, h ^ 1) for h in range(heads)]
    at_low = place <= low
    partials = [product(columns(core, at_low), columns(1 - core, at_low))]
    for j in range(1, toks):
        piece = lax.ppermute(
            columns(core, place == line[j]), "tok", [(line[j], low), (mirror[j], high)]
        )
        partials.append(product(piece, lax.ppermute(piece, "head", cores)))
    over = [
        (flat(high, h), flat(low, h)) if h % 2 == 0 else (flat(low, h), flat(high, h))
        for h in range(heads)
    ]
    others = [lax.ppermute(partial_sum, both, over) for partial_sum in partials]

    da, db, dots, dq = call_query(
        slots, partials, others, swap, sums, entries, wa, wb, ga, gb
    )
    dots = exchange(dots)
    is_root = place == jnp.where(core == 0, low, high)

    def home(slot_outs):
        back = None
        for j in range(1, toks):
            got = lax.ppermute(slot_outs[j], both, from_root(j))
            back = got if back is None else back + got
        return jnp.where(is_root, slot_outs[0], back)

    d_queries = home(dq)
    first = toks // 2
    outs_far = call_key(
        slots[first:], sums, dots, entries, first, key_gain, wa, wb, ga, gb, da, db, *kept
    )
    outs_near = call_key(
        slots[:first], sums, dots, entries, 0, key_gain, wa, wb, ga, gb, da, db, *kept
    )
    pair = home(list(outs_near) + list(outs_far))
    return d_queries, pair[:, :width], pair[:, width:]


def call(kernel, name, units, rows, out_shape, out_specs, operands, scratch):
    light = name == "gradient"
    return pl.pallas_call(
        kernel,
        out_shape=out_shape,
        in_specs=[spec for _, spec in operands],
        out_specs=out_specs,
        scratch_shapes=scratch,
        compiler_params=pltpu.CompilerParams(vmem_limit_bytes=vmem_bytes),
        cost_estimate=estimate(0.01 if light else units, rows),
        name=name,
    )(*(value for value, _ in operands))


def held_rows(count, rows, columns, dtype):
    return [pltpu.VMEM((count * rows, columns), dtype), pltpu.SemaphoreType.DMA((count,))]


def gradient_kernel(count, *refs):
    slots = refs[:count]
    gain_ref, wa_ref, wb_ref, g_ref, sq_ref, kept, held, sems, misfit, sem_m = refs[count:]
    wait = fetch(slots, held, sems)
    gain = gain_ref[0]
    width, rows = wb_ref.shape[0], slots[0].shape[0]
    g_ref[...] = jnp.zeros_like(g_ref)

    @pl.loop(0, count)
    def _(j):
        wait(j)
        here = part(j, rows)
        keys = held[here, :width]
        values = held[here, width : 2 * width].astype(f32)
        mixed = nn(keys, wa_ref[...]) * gain
        u, w = mixed[:, :width], mixed[:, width:]
        sg = sigmoid(u)
        act = u * sg
        hidden = halves(act * w)
        e = two(nn, hidden, wb_ref[...]) - values
        misfit[here, :width] = e
        e2 = halves(e)
        hb = two(nt, e2, wb_ref[...])
        misfit[here, width:] = hb
        pltpu.make_async_copy(misfit.at[here], kept.at[here], sem_m.at[j]).start()
        g_ref[:, 2 * width :] += three(tn, hidden, e2)
        slope = sg * (1.0 + u * (1.0 - sg))
        g_ref[:, :width] += two_right(tn, keys, halves(hb * w * slope))
        g_ref[:, width : 2 * width] += two_right(tn, keys, halves(hb * act))

    ga = g_ref[:, : 2 * width] * gain
    g_ref[:, : 2 * width] = ga
    gb = g_ref[:, 2 * width :]
    sq_ref[...] = jnp.zeros_like(sq_ref) + (jnp.sum(ga * ga) + jnp.sum(gb * gb))
    for j in range(count):
        here = part(j, rows)
        pltpu.make_async_copy(misfit.at[here], kept.at[here], sem_m.at[j]).wait()


def call_gradient(slots, gain, wa, wb):
    count, (rows, columns) = len(slots), slots[0].shape
    width = wb.shape[0]
    return call(
        partial(gradient_kernel, count),
        "gradient",
        13,
        rows * count,
        (shape_of(width, 3 * width), shape_of(8, 128), shape_of(count * rows, 2 * width)),
        [vmem_spec(), vmem_spec(), any_spec()],
        [(x, any_spec()) for x in slots]
        + [(gain, smem_spec()), (wa, vmem_spec()), (wb, vmem_spec())],
        held_rows(count, rows, columns, bf16) + held_rows(count, rows, 2 * width, f32),
    )


def pull_query_kernel(opening, entries, *refs):
    slots, own, other = refs[:2], refs[2:4], refs[4:6]
    if opening:
        g_all, sum0, sum1, wa_ref, wb_ref, acc_ref, uh, ul, dq0, dq1 = refs[6:16]
    else:
        g_all, old, uh, ul, acc_ref, p_ref, mh, ml = refs[6:14]
    held, sem_q, left, sem_l, right, sem_r, g_ref, sem_g, sem_a = refs[-9:]
    width, rows = held.shape[1], slots[0].shape[0]
    both_in, gate, up, down = (
        slice(0, 2 * width),
        slice(0, width),
        slice(width, 2 * width),
        slice(2 * width, 3 * width),
    )
    waits = [
        fetch([block.at[:, down] for block in slots], held, sem_q),
        fetch(own, left, sem_l),
        fetch(other, right, sem_r),
    ]
    g_wait = fetch([g_all], g_ref, sem_g)
    if opening:
        g_wait(0)
        _, scale = scale_of((sum0, sum1), entries)
        rate = inner_rate / scale
        for w_ref, place in ((wa_ref, both_in), (wb_ref, down)):
            uh[:, place], ul[:, place] = halves(w_ref[...].astype(f32) - g_ref[:, place] * rate)
        acc_ref[...] = jnp.zeros_like(acc_ref)
    else:
        a_wait = fetch([old], acc_ref, sem_a)

    @pl.loop(0, 2)
    def _(j):
        for wait in waits:
            wait(j)
        here = part(j, rows)
        queries = held[here]
        d_out = halves(left[here] + right[here])
        mixed = two_right(nn, queries, (uh[:, both_in], ul[:, both_in]))
        u, w = mixed[:, :width], mixed[:, width:]
        sg = sigmoid(u)
        act = u * sg
        hb = three(nt, d_out, (uh[:, down], ul[:, down]))
        if not opening:

            @pl.when(j == 0)
            def _():
                a_wait(0)

        acc_ref[:, down] += three(tn, halves(act * w), d_out)
        slope = sg * (1.0 + u * (1.0 - sg))
        ub = halves(hb * w * slope)
        wbar = halves(hb * act)
        acc_ref[:, gate] += two_right(tn, queries, ub)
        acc_ref[:, up] += two_right(tn, queries, wbar)
        if not opening:
            for m_ref, gate_part, up_part in ((mh, ub[0], wbar[0]), (ml, ub[1], wbar[1])):
                m_ref[here, :width] = gate_part
                m_ref[here, width:] = up_part
            return
        back = three(nt, ub, (uh[:, gate], ul[:, gate])) + three(
            nt, wbar, (uh[:, up], ul[:, up])
        )
        for k, dq_ref in enumerate((dq0, dq1)):

            @pl.when(j == k)
            def _():
                dq_ref[...] = back.astype(bf16)

    if not opening:
        g_wait(0)
        p_ref[...] = jnp.zeros_like(p_ref) + jnp.sum(g_ref[...] * acc_ref[...])


def query_grad_kernel(mh, ml, uh, ul, *dqs):
    width = uh.shape[0]
    rows = mh.shape[0] // 2
    both_in = slice(0, 2 * width)
    for k, dq_ref in enumerate(dqs):
        here = slice(k * rows, (k + 1) * rows)
        back = three(nt, (mh[here], ml[here]), (uh[:, both_in], ul[:, both_in]))
        dq_ref[...] = back.astype(bf16)


def call_query_grad(mh, ml, uh, ul):
    rows, width = mh.shape[0] // 2, uh.shape[0]
    return call(
        query_grad_kernel,
        "query_grad",
        6,
        2 * rows,
        (shape_of(rows, width, dtype=bf16),) * 2,
        [vmem_spec()] * 2,
        [(x, vmem_spec()) for x in (mh, ml, uh, ul)],
        [],
    )


def call_pull_query(entries, slots, own, other, streams, more, opening):
    rows, width = slots[0].shape[0], slots[0].shape[1] // 3
    whole = shape_of(width, 3 * width)
    half = shape_of(width, 3 * width, dtype=bf16)
    dq = shape_of(rows, width, dtype=bf16)
    mixed = shape_of(2 * rows, 2 * width, dtype=bf16)
    outs = (whole, half, half, dq, dq) if opening else (whole, shape_of(8, 128), mixed, mixed)
    return call(
        partial(pull_query_kernel, opening, entries),
        "query_pull",
        20,
        rows * 2,
        outs,
        [vmem_spec()] * len(outs),
        [(x, any_spec()) for x in (*slots, *own, *other, *streams)]
        + [(x, vmem_spec()) for x in more],
        held_rows(2, rows, width, bf16)
        + held_rows(2, rows, width, f32)
        + held_rows(2, rows, width, f32)
        + held_rows(1, width, 3 * width, f32)
        + [pltpu.SemaphoreType.DMA((1,))],
    )


def pull_key_kernel(entries, blocks, *refs):
    count = len(blocks)
    slots, refs = refs[:count], refs[count:]
    kept, gain_ref, wa_ref, wb_ref = refs[:4]
    sum0, sum1, dot0, dot1, g_ref, du_ref = refs[4:10]
    out, scratch = refs[10 : 10 + count], refs[10 + count :]
    held, sem_k, kept_held, sem_e, dh, dl = scratch
    width, rows = wb_ref.shape[0], slots[0].shape[0]
    waits = [
        fetch(slots, held, sem_k),
        fetch([kept.at[part(block, rows)] for block in blocks], kept_held, sem_e),
    ]
    gain = gain_ref[0]
    rms, scale = scale_of((sum0, sum1), entries)
    pull = (dot0[0:1, 0:1] + dot1[0:1, 0:1]) / (scale * scale * entries * rms)
    dh[...], dl[...] = halves((du_ref[...] * (1.0 / scale) - g_ref[...] * pull) * (-inner_rate))
    both_in, gate, up, down = (
        slice(0, 2 * width),
        slice(0, width),
        slice(width, 2 * width),
        slice(2 * width, 3 * width),
    )

    @pl.loop(0, count)
    def _(j):
        for wait in waits:
            wait(j)
        here = part(j, rows)
        keys = held[here, :width]
        mixed = nn(keys, wa_ref[...]) * gain
        moved = two_right(nn, keys, (dh[:, both_in], dl[:, both_in])) * gain
        u, w = mixed[:, :width], mixed[:, width:]
        du, dw = moved[:, :width], moved[:, width:]
        sg = sigmoid(u)
        act = u * sg
        rest = 1.0 - sg
        slope = sg * (1.0 + u * rest)
        bend = sg * rest * (2.0 + u * (rest - sg))
        db = (dh[:, down], dl[:, down])
        shift = two(nn, halves(slope * du * w + act * dw), wb_ref[...]) + three(
            nn, halves(act * w), db
        )
        back = two(nt, halves(shift), wb_ref[...]) + three(
            nt, halves(kept_held[here, :width]), db
        )
        hb = kept_held[here, width:]
        ub = halves(back * w * slope + hb * (bend * du * w + slope * dw))
        wbar = halves(back * act + hb * slope * du)
        ut = halves(hb * slope * w)
        wt = halves(hb * act)
        grad = (
            two(nt, ub, wa_ref[:, :width])
            + two(nt, wbar, wa_ref[:, width:])
            + three(nt, ut, (dh[:, gate], dl[:, gate]))
            + three(nt, wt, (dh[:, up], dl[:, up]))
        )
        for k, out_ref in enumerate(out):

            @pl.when(j == k)
            def _():
                out_ref[:, :width] = (grad * gain).astype(bf16)
                out_ref[:, width:] = (-shift).astype(bf16)


def call_pull_key(blocks, entries, slots, kept, gain, wa, wb, terms):
    count, (rows, columns) = len(blocks), slots[0].shape
    width = wb.shape[0]
    return call(
        partial(pull_key_kernel, entries, blocks),
        "key_pull",
        26,
        rows * count,
        (shape_of(rows, 2 * width, dtype=bf16),) * count,
        [vmem_spec()] * count,
        [(slots[block], any_spec()) for block in blocks]
        + [(kept, any_spec()), (gain, smem_spec()), (wa, vmem_spec()), (wb, vmem_spec())]
        + [(x, vmem_spec()) for x in terms],
        held_rows(count, rows, columns, bf16)
        + held_rows(count, rows, 2 * width, f32)
        + [pltpu.VMEM((width, 3 * width), bf16)] * 2,
    )


def four_line(queries, keys, values, fast_in, fast_out, key_gain, out_proj, grad_out):
    toks, heads = 4, lax.axis_size("head")
    low, high = 1, 2
    width = fast_out.shape[1]
    entries = float(heads * (fast_in.shape[1] * fast_in.shape[2] + width * fast_out.shape[2]))
    place, head = lax.axis_index("tok"), lax.axis_index("head")
    core = lax.rem(head, 2)
    line, mirror = (1, 0, 2, 3), (2, 3, 1, 0)
    both = ("tok", "head")
    tie = lax.optimization_barrier

    def flat(t, h):
        return t * heads + h

    def root(h):
        return high if h % 2 else low

    def order(h):
        return mirror if h % 2 else line

    def to_root(j):
        return [(flat(order(h)[j], h), flat(root(h), h)) for h in range(heads)]

    def home(value, j):
        return lax.ppermute(value, both, [(b, a) for a, b in to_root(j)])

    is_root = place == jnp.where(core == 0, low, high)
    wa, wb = fast_in[0], fast_out[0]
    rows_in = jnp.concatenate([keys, values, queries], axis=1)
    slots = [rows_in] + [lax.ppermute(rows_in, both, to_root(j)) for j in range(1, toks)]

    group, half = lax.axis_index("groups"), out_proj.shape[0] // 2
    far_half = lax.ppermute(
        lax.dynamic_slice_in_dim(out_proj, group * half, half, axis=0),
        "tok",
        [(0, low), (3, high)],
    )
    quarter = grad_out.shape[1] // 4

    def columns(array, which, half_is_low):
        index = jnp.where(half_is_low, 1 - which, 2 + which)
        return lax.dynamic_slice_in_dim(array, index * quarter, quarter, axis=1)

    def piece(array, j):
        return lax.ppermute(
            columns(array, core, place == line[j]), "tok", [(line[j], low), (mirror[j], high)]
        )

    def swap_cores(value):
        return lax.ppermute(value, "head", [(h, h ^ 1) for h in range(heads)])

    piece2 = piece(grad_out, 2)
    later, far_half, piece2, *slots = tie((grad_out, far_half, piece2, *slots))
    far_other = lax.ppermute(far_half, "groups", [(0, 1), (1, 0)])

    def exchange(value, pairs, step_pairs, beside=None):
        more = lax.ppermute(value, both, pairs)
        if beside is not None:
            outs, more = tie((beside(), more))
        value = value + more
        step = 2
        while True:
            more = lax.ppermute(value, both, step_pairs(step))
            step *= 2
            if step >= heads:
                return (value, more) if beside is None else (value, more, outs)
            value = value + more

    over = [
        (flat(high, h), flat(low, h)) if h % 2 == 0 else (flat(low, h), flat(high, h))
        for h in range(heads)
    ]
    root_pairs = [(flat(root(h), h), flat(root(h ^ 1), h ^ 1)) for h in range(heads)]

    def root_steps(step):
        return [(flat(root(h), h), flat(root(h), h ^ step)) for h in range(heads)]

    at_low = place <= low
    piece3 = piece(later, 3)
    piece1 = piece(later, 1)
    g, squares, kept = call_gradient(slots, key_gain, wa, wb)
    g, squares, far_half, far_other, piece2, mine0, theirs0 = tie(
        (
            g,
            squares,
            far_half,
            far_other,
            piece2,
            columns(later, core, at_low),
            columns(later, 1 - core, at_low),
        )
    )

    far = jnp.where(
        group == 0,
        jnp.concatenate([far_half, far_other], axis=0),
        jnp.concatenate([far_other, far_half], axis=0),
    )
    w_mine = jnp.where(core == 0, out_proj, far)
    w_theirs = jnp.where(core == 0, far, out_proj)

    def product(mine, theirs):
        return nt(mine, w_mine) + nt(theirs, w_theirs)

    own0 = product(mine0, theirs0)
    other2 = lax.ppermute(own0, both, over)
    own2 = product(piece2, swap_cores(piece2))
    other0 = lax.ppermute(own2, both, over)
    squares_in, *_ = tie((squares, own0, own2))
    sums = exchange(squares_in, root_pairs, root_steps)
    piece3, piece1, other0, other2, *sums = tie((piece3, piece1, other0, other2, *sums))

    own3 = product(piece3, swap_cores(piece3))
    other1 = lax.ppermute(own3, both, over)
    own1 = product(piece1, swap_cores(piece1))
    other3 = lax.ppermute(own1, both, over)
    own3, own1, *sums = tie((own3, own1, *sums))
    acc, uh, ul, dq0, dq2 = call_pull_query(
        entries, slots[0::2], (own0, own2), (other0, other2), (g,), (*sums, wa, wb), True
    )
    other1, other3, acc, uh, ul, dq2 = tie((other1, other3, acc, uh, ul, dq2))

    du, dots, mh, ml = call_pull_query(
        entries, slots[1::2], (own1, own3), (other1, other3), (g, acc), (uh, ul), False
    )
    du, dots, mh, ml = tie((du, dots, mh, ml))

    *dots, (dq1, dq3) = exchange(
        dots, root_pairs, root_steps, lambda: call_query_grad(mh, ml, uh, ul)
    )
    du, dq1, dq3, *dots = tie((du, dq1, dq3, *dots))

    terms = (*sums, *dots, g, du)
    dq1, dq2, dq3 = home(dq1, 1), home(dq2, 2), home(dq3, 3)
    out3, out2 = call_pull_key((3, 2), entries, slots, kept, key_gain, wa, wb, terms)
    out3, out2, dq1, dq2, dq3, *terms = tie((out3, out2, dq1, dq2, dq3, *terms))

    out3, out2 = home(out3, 3), home(out2, 2)
    out1, out0 = call_pull_key((1, 0), entries, slots, kept, key_gain, wa, wb, terms)
    d_queries = jnp.where(is_root, dq0, dq1 + dq2 + dq3)
    out3, out2, out1, out0, d_queries = tie((out3, out2, out1, out0, d_queries))

    pair = jnp.where(is_root, out0, home(out1, 1) + out2 + out3)
    return d_queries, pair[:, :width], pair[:, width:]


def per_device(*arrays):
    fits = lax.axis_size("tok") == 4 and lax.axis_size("head") >= 4 and lax.axis_size("groups") == 2
    return (four_line if fits else any_line)(*arrays)


def solution(mesh):
    rows = P(("groups", "tok"), "head")
    return jax.shard_map(
        per_device,
        mesh=mesh,
        in_specs=(
            rows,
            rows,
            rows,
            P("head", None, None),
            P("head", None, None),
            P("head"),
            P("head", "tok"),
            P(("groups", "tok"), None),
        ),
        out_specs=(rows, rows, rows),
        check_vma=False,
    )
```

```python
from functools import partial

import jax
import jax.numpy as jnp
from jax import lax
from jax.experimental import pallas as pl
from jax.experimental.pallas import tpu as pltpu
from jax.sharding import PartitionSpec as P

f32 = jnp.float32
bf16 = jnp.bfloat16
inner_rate = 0.02
norm_eps = 1e-06
vmem_bytes = 56 * 1024 * 1024
MIB = 1024 * 1024
JOIN = 1


def halves(x):
    top = x.astype(bf16)
    return top, (x - top.astype(f32)).astype(bf16)


def nn(a, b):
    return lax.dot_general(a, b, (((1,), (0,)), ((), ())), preferred_element_type=f32)


def nt(a, b):
    return lax.dot_general(a, b, (((1,), (1,)), ((), ())), preferred_element_type=f32)


def tn(a, b):
    return lax.dot_general(a, b, (((0,), (0,)), ((), ())), preferred_element_type=f32)


def joined(dot, a, b):
    left, right = {nn: (1, 0), nt: (1, 1), tn: (0, 0)}[dot]
    return dot(jnp.concatenate(a, axis=left), jnp.concatenate(b, axis=right))


def two(dot, a, b):
    return joined(dot, a, (b, b))


def two_right(dot, a, b):
    return joined(dot, (a, a), b)


def three(dot, a, b):
    return joined(dot, (a[0], a[0], a[1]), (b[0], b[1], b[0]))


def sigmoid(u):
    return 1.0 / (1.0 + jnp.exp(-u))


def part(j, rows):
    return pl.ds(pl.multiple_of(j * rows, rows), rows)


def fetch(sources, held, sems):
    rows = held.shape[0] // len(sources)
    for j, source in enumerate(sources):
        pltpu.make_async_copy(source, held.at[part(j, rows)], sems.at[j]).start()

    def wait(j):
        pltpu.make_async_copy(sources[0], held.at[part(j, rows)], sems.at[j]).wait()

    return wait


def joined_loop(count, rows, waits, body):
    join = JOIN
    while count % join:
        join -= 1

    @pl.loop(0, count // join)
    def _(i):
        for wait in waits:
            for k in range(join):
                wait(i * join + k)
        body(part(i, rows * join))


def inner_grad_kernel(count, keep, *refs):
    slots = refs[:count]
    gain_ref, wa_ref, wb_ref, ga_ref, gb_ref, sq_ref = refs[count : count + 6]
    held, sems = refs[-2:]
    wait = fetch(slots, held, sems)
    gain = gain_ref[0]
    width = wb_ref.shape[0]
    ga_ref[...] = jnp.zeros_like(ga_ref)
    gb_ref[...] = jnp.zeros_like(gb_ref)

    def body(j):
        keys = held[j, :width]
        values = held[j, width : 2 * width].astype(f32)
        mixed = nn(keys, wa_ref[...]) * gain
        u, w = mixed[:, :width], mixed[:, width:]
        sg = sigmoid(u)
        act = u * sg
        hidden = halves(act * w)
        e = two(nn, hidden, wb_ref[...]) - values
        e2 = halves(e)
        hb = two(nt, e2, wb_ref[...])
        if keep:
            e_ref, hb_ref = refs[count + 6 : count + 8]
            e_ref[j] = e
            hb_ref[j] = hb
        gb_ref[...] += three(tn, hidden, e2)
        slope = sg * (1.0 + u * (1.0 - sg))
        ga_ref[:, :width] += two_right(tn, keys, halves(hb * w * slope))
        ga_ref[:, width:] += two_right(tn, keys, halves(hb * act))

    joined_loop(count, slots[0].shape[0], [wait], body)
    ga = ga_ref[...] * gain
    ga_ref[...] = ga
    gb = gb_ref[...]
    sq_ref[...] = jnp.zeros_like(sq_ref) + (jnp.sum(ga * ga) + jnp.sum(gb * gb))


def vmem_spec():
    return pl.BlockSpec(memory_space=pltpu.VMEM)


def any_spec():
    return pl.BlockSpec(memory_space=pl.ANY)


def smem_spec():
    return pl.BlockSpec(memory_space=pltpu.SMEM)


def shape_of(*dims, dtype=f32):
    return jax.ShapeDtypeStruct(dims, dtype)


def estimate(units, rows):
    return pl.CostEstimate(
        flops=int(units * 2 * rows * 512 * 512), bytes_accessed=MIB, transcendentals=0
    )


def call_inner_grad(slots, keep, gain, wa, wb):
    count = len(slots)
    kept = 2 if keep else 0
    rows, width = slots[0].shape[0], wb.shape[0]
    return pl.pallas_call(
        partial(inner_grad_kernel, count, keep),
        out_shape=(shape_of(width, 2 * width), shape_of(width, width), shape_of(8, 128))
        + (shape_of(count * rows, width),) * kept,
        in_specs=[any_spec()] * count + [smem_spec(), vmem_spec(), vmem_spec()],
        out_specs=[vmem_spec()] * (3 + kept),
        scratch_shapes=[
            pltpu.VMEM((count * rows, slots[0].shape[1]), bf16),
            pltpu.SemaphoreType.DMA((count,)),
        ],
        compiler_params=pltpu.CompilerParams(vmem_limit_bytes=vmem_bytes),
        cost_estimate=estimate(13, rows * count),
        name="inner_grad",
    )(*slots, gain, wa, wb)


def scale_of(sums, entries):
    total = sums[0][0:1, 0:1]
    for more in sums[1:]:
        total = total + more[0:1, 0:1]
    rms = jnp.sqrt(total / entries)
    return rms, rms + norm_eps


def query_kernel(count, n_sums, entries, swap, *refs):
    slots, refs = refs[:count], refs[count:]
    own, refs = refs[:count], refs[count:]
    other, refs = refs[:count], refs[count:]
    sums, refs = refs[:n_sums], refs[n_sums:]
    (wa_ref, wb_ref, ga_ref, gb_ref), refs = refs[:4], refs[4:]
    (da_ref, db_ref, p_ref), refs = refs[:3], refs[3:]
    dq, refs = refs[:count], refs[count:]
    held, left, right, ah, al, bh, bl, dq_held, sem_q, sem_l, sem_r, sem_o = refs
    width = wb_ref.shape[0]
    waits = [
        fetch([slot.at[:, 2 * width : 3 * width] for slot in slots], held, sem_q),
        fetch(own, left, sem_l),
        fetch([other[swap[j]] for j in range(count)], right, sem_r),
    ]
    _, scale = scale_of(sums, entries)
    rate = inner_rate / scale
    ah[...], al[...] = halves(wa_ref[...].astype(f32) - ga_ref[...] * rate)
    bh[...], bl[...] = halves(wb_ref[...].astype(f32) - gb_ref[...] * rate)
    da_ref[...] = jnp.zeros_like(da_ref)
    db_ref[...] = jnp.zeros_like(db_ref)

    def body(j):
        queries = held[j]
        d_out = halves(left[j] + right[j])
        a = (ah[...], al[...])
        b = (bh[...], bl[...])
        mixed = two_right(nn, queries, a)
        u, w = mixed[:, :width], mixed[:, width:]
        sg = sigmoid(u)
        act = u * sg
        hb = three(nt, d_out, b)
        db_ref[...] += three(tn, halves(act * w), d_out)
        slope = sg * (1.0 + u * (1.0 - sg))
        ub = halves(hb * w * slope)
        wbar = halves(hb * act)
        da_ref[:, :width] += two_right(tn, queries, ub)
        da_ref[:, width:] += two_right(tn, queries, wbar)
        back = three(nt, ub, (ah[:, :width], al[:, :width])) + three(
            nt, wbar, (ah[:, width:], al[:, width:])
        )
        dq_held[j] = back.astype(bf16)

    rows = slots[0].shape[0]
    joined_loop(count, rows, waits, body)
    copies = [
        pltpu.make_async_copy(dq_held.at[part(j, rows)], dq[j], sem_o.at[j]) for j in range(count)
    ]
    for copy in copies:
        copy.start()
    total = jnp.sum(ga_ref[...] * da_ref[...]) + jnp.sum(gb_ref[...] * db_ref[...])
    p_ref[...] = jnp.zeros_like(p_ref) + total
    for copy in copies:
        copy.wait()


def call_query(slots, own, other, swap, sums, entries, wa, wb, ga, gb):
    count = len(slots)
    rows, width = slots[0].shape[0], wb.shape[0]
    outs = pl.pallas_call(
        partial(query_kernel, count, len(sums), entries, swap),
        out_shape=(shape_of(width, 2 * width), shape_of(width, width), shape_of(8, 128))
        + (shape_of(rows, width, dtype=bf16),) * count,
        in_specs=[any_spec()] * (3 * count) + [vmem_spec()] * (len(sums) + 4),
        out_specs=[vmem_spec()] * 3 + [any_spec()] * count,
        scratch_shapes=[
            pltpu.VMEM((count * rows, width), bf16),
            pltpu.VMEM((count * rows, width), f32),
            pltpu.VMEM((count * rows, width), f32),
            pltpu.VMEM((width, 2 * width), bf16),
            pltpu.VMEM((width, 2 * width), bf16),
            pltpu.VMEM((width, width), bf16),
            pltpu.VMEM((width, width), bf16),
            pltpu.VMEM((count * rows, width), bf16),
            pltpu.SemaphoreType.DMA((count,)),
            pltpu.SemaphoreType.DMA((count,)),
            pltpu.SemaphoreType.DMA((count,)),
            pltpu.SemaphoreType.DMA((count,)),
        ],
        compiler_params=pltpu.CompilerParams(vmem_limit_bytes=vmem_bytes),
        cost_estimate=estimate(20, rows * count),
        name="query_pull",
    )(*slots, *own, *other, *sums, wa, wb, ga, gb)
    return outs[0], outs[1], outs[2], outs[3:]


def key_kernel(count, n_sums, n_kept, entries, first, *refs):
    slots, refs = refs[:count], refs[count:]
    sums, refs = refs[:n_sums], refs[n_sums:]
    dots, refs = refs[:n_sums], refs[n_sums:]
    gain_ref, wa_ref, wb_ref, ga_ref, gb_ref, da_ref, db_ref = refs[:7]
    refs = refs[7:]
    kept, refs = refs[:n_kept], refs[n_kept:]
    out, refs = refs[:count], refs[count:]
    held, dah, dal, dbh, dbl, out_held, sem_k, sem_o = refs[:8]
    kept_held, kept_sems = refs[8 : 8 + n_kept], refs[8 + n_kept :]
    width = wb_ref.shape[0]
    rows = slots[0].shape[0]
    waits = [fetch(slots, held, sem_k)]
    for source, target, sems in zip(kept, kept_held, kept_sems):
        waits.append(
            fetch([source.at[part(first + j, rows)] for j in range(count)], target, sems)
        )
    gain = gain_ref[0]
    rms, scale = scale_of(sums, entries)
    product = dots[0][0:1, 0:1]
    for more in dots[1:]:
        product = product + more[0:1, 0:1]
    pull = product / (scale * scale * entries * rms)
    for d_ref, g_ref, h_ref, l_ref in (
        (da_ref, ga_ref, dah, dal),
        (db_ref, gb_ref, dbh, dbl),
    ):
        h_ref[...], l_ref[...] = halves(
            (d_ref[...] * (1.0 / scale) - g_ref[...] * pull) * (-inner_rate)
        )

    def body(j):
        keys = held[j, :width]
        mixed = nn(keys, wa_ref[...]) * gain
        moved = two_right(nn, keys, (dah[...], dal[...])) * gain
        u, w = mixed[:, :width], mixed[:, width:]
        du, dw = moved[:, :width], moved[:, width:]
        sg = sigmoid(u)
        act = u * sg
        rest = 1.0 - sg
        slope = sg * (1.0 + u * rest)
        bend = sg * rest * (2.0 + u * (rest - sg))
        db = (dbh[...], dbl[...])
        hidden = halves(act * w)
        shift = two(nn, halves(slope * du * w + act * dw), wb_ref[...]) + three(nn, hidden, db)
        out_held[j, width:] = (-shift).astype(bf16)
        if n_kept:
            e2, hb = halves(kept_held[0][j]), kept_held[1][j]
        else:
            values = held[j, width : 2 * width].astype(f32)
            e2 = halves(two(nn, hidden, wb_ref[...]) - values)
            hb = two(nt, e2, wb_ref[...])
        back = two(nt, halves(shift), wb_ref[...]) + three(nt, e2, db)
        ub = halves(back * w * slope + hb * (bend * du * w + slope * dw))
        wbar = halves(back * act + hb * slope * du)
        ut = halves(hb * slope * w)
        wt = halves(hb * act)
        grad = (
            two(nt, ub, wa_ref[:, :width])
            + two(nt, wbar, wa_ref[:, width:])
            + three(nt, ut, (dah[:, :width], dal[:, :width]))
            + three(nt, wt, (dah[:, width:], dal[:, width:]))
        )
        out_held[j, :width] = (grad * gain).astype(bf16)

    joined_loop(count, rows, waits, body)
    copies = [
        pltpu.make_async_copy(out_held.at[part(j, rows)], out[j], sem_o.at[j]) for j in range(count)
    ]
    for copy in copies:
        copy.start()
    for copy in copies:
        copy.wait()


def call_key(slots, sums, dots, entries, first, gain, wa, wb, ga, gb, da, db, *kept):
    count = len(slots)
    rows, width = slots[0].shape[0], wb.shape[0]
    return pl.pallas_call(
        partial(key_kernel, count, len(sums), len(kept), entries, first),
        out_shape=(shape_of(rows, 2 * width, dtype=bf16),) * count,
        in_specs=[any_spec()] * count
        + [vmem_spec()] * (2 * len(sums))
        + [smem_spec()]
        + [vmem_spec()] * 6
        + [any_spec()] * len(kept),
        out_specs=[any_spec()] * count,
        scratch_shapes=[
            pltpu.VMEM((count * rows, slots[0].shape[1]), bf16),
            pltpu.VMEM((width, 2 * width), bf16),
            pltpu.VMEM((width, 2 * width), bf16),
            pltpu.VMEM((width, width), bf16),
            pltpu.VMEM((width, width), bf16),
            pltpu.VMEM((count * rows, 2 * width), bf16),
            pltpu.SemaphoreType.DMA((count,)),
            pltpu.SemaphoreType.DMA((count,)),
        ]
        + [pltpu.VMEM((count * rows, width), f32)] * len(kept)
        + [pltpu.SemaphoreType.DMA((count,))] * len(kept),
        compiler_params=pltpu.CompilerParams(vmem_limit_bytes=vmem_bytes),
        cost_estimate=estimate(26, rows * count),
        name="key_pull",
    )(*slots, *sums, *dots, gain, wa, wb, ga, gb, da, db, *kept)


def any_line(queries, keys, values, fast_in, fast_out, key_gain, out_proj, grad_out):
    toks, heads = lax.axis_size("tok"), lax.axis_size("head")
    low, high = toks // 2 - 1, toks // 2
    width = fast_out.shape[1]
    entries = float(heads * (fast_in.shape[1] * fast_in.shape[2] + width * fast_out.shape[2]))
    wa, wb = fast_in[0], fast_out[0]
    place, head = lax.axis_index("tok"), lax.axis_index("head")
    core = lax.rem(head, 2)
    line = sorted(range(toks), key=lambda t: (abs(t - low), t))
    mirror = [toks - 1 - t for t in line]
    swap = tuple(mirror.index(t) for t in line)

    def root(h):
        return high if h % 2 else low

    def flat(t, h):
        return t * heads + h

    both = ("tok", "head")

    def to_root(j):
        return [(flat((mirror if h % 2 else line)[j], h), flat(root(h), h)) for h in range(heads)]

    def from_root(j):
        return [(b, a) for a, b in to_root(j)]

    rows_in = jnp.concatenate([keys, values, queries], axis=1)
    slots = [rows_in] + [lax.ppermute(rows_in, both, to_root(j)) for j in range(1, toks)]

    ga, gb, squares, *kept = call_inner_grad(slots, toks <= 8, key_gain, wa, wb)

    def exchange(value):
        parts = [value]
        for step in range(1, heads):
            turn = [(h, (h + step) % heads) for h in range(heads)]
            parts.append(
                lax.ppermute(value, both, [(flat(root(a), a), flat(root(b), b)) for a, b in turn])
            )
        return parts

    sums = exchange(squares)

    blocks = [out_proj] + [
        lax.ppermute(out_proj, "tok", [(low - j, low), (high + j, high)])
        for j in range(1, toks // 2)
    ]
    quarter = grad_out.shape[1] // 4

    def side_of(parts):
        if len(parts) == 1:
            return parts[0]
        return jnp.where(
            place <= low, jnp.concatenate(parts[::-1], axis=1), jnp.concatenate(parts, axis=1)
        )

    near, far = side_of(blocks[: toks // 4]), side_of(blocks[toks // 4 :])
    w_mine = jnp.where(core == 0, near, far)
    w_theirs = jnp.where(core == 0, far, near)

    def columns(which, half_is_low):
        index = jnp.where(half_is_low, 1 - which, 2 + which)
        return lax.dynamic_slice_in_dim(grad_out, index * quarter, quarter, axis=1)

    def product(mine, theirs):
        return (
            lax.dot_general(mine, w_mine, (((1,), (1,)), ((), ())), preferred_element_type=f32)
            + lax.dot_general(
                theirs, w_theirs, (((1,), (1,)), ((), ())), preferred_element_type=f32
            )
        )

    cores = [(h, h ^ 1) for h in range(heads)]
    at_low = place <= low
    partials = [product(columns(core, at_low), columns(1 - core, at_low))]
    for j in range(1, toks):
        piece = lax.ppermute(
            columns(core, place == line[j]), "tok", [(line[j], low), (mirror[j], high)]
        )
        partials.append(product(piece, lax.ppermute(piece, "head", cores)))
    over = [
        (flat(high, h), flat(low, h)) if h % 2 == 0 else (flat(low, h), flat(high, h))
        for h in range(heads)
    ]
    others = [lax.ppermute(partial_sum, both, over) for partial_sum in partials]

    da, db, dots, dq = call_query(
        slots, partials, others, swap, sums, entries, wa, wb, ga, gb
    )
    dots = exchange(dots)
    is_root = place == jnp.where(core == 0, low, high)

    def home(slot_outs):
        back = None
        for j in range(1, toks):
            got = lax.ppermute(slot_outs[j], both, from_root(j))
            back = got if back is None else back + got
        return jnp.where(is_root, slot_outs[0], back)

    d_queries = home(dq)
    first = toks // 2
    outs_far = call_key(
        slots[first:], sums, dots, entries, first, key_gain, wa, wb, ga, gb, da, db, *kept
    )
    outs_near = call_key(
        slots[:first], sums, dots, entries, 0, key_gain, wa, wb, ga, gb, da, db, *kept
    )
    pair = home(list(outs_near) + list(outs_far))
    return d_queries, pair[:, :width], pair[:, width:]


def call(kernel, name, units, rows, out_shape, out_specs, operands, scratch):
    light = name == "gradient"
    return pl.pallas_call(
        kernel,
        out_shape=out_shape,
        in_specs=[spec for _, spec in operands],
        out_specs=out_specs,
        scratch_shapes=scratch,
        compiler_params=pltpu.CompilerParams(vmem_limit_bytes=vmem_bytes),
        cost_estimate=estimate(0.01 if light else units, rows),
        name=name,
    )(*(value for value, _ in operands))


def held_rows(count, rows, columns, dtype):
    return [pltpu.VMEM((count * rows, columns), dtype), pltpu.SemaphoreType.DMA((count,))]


def gradient_kernel(count, *refs):
    slots = refs[:count]
    gain_ref, wa_ref, wb_ref, g_ref, sq_ref, kept, held, sems, misfit, sem_m = refs[count:]
    wait = fetch(slots, held, sems)
    gain = gain_ref[0]
    width, rows = wb_ref.shape[0], slots[0].shape[0]
    g_ref[...] = jnp.zeros_like(g_ref)

    @pl.loop(0, count)
    def _(j):
        wait(j)
        here = part(j, rows)
        keys = held[here, :width]
        values = held[here, width : 2 * width].astype(f32)
        mixed = nn(keys, wa_ref[...]) * gain
        u, w = mixed[:, :width], mixed[:, width:]
        sg = sigmoid(u)
        act = u * sg
        hidden = halves(act * w)
        e = two(nn, hidden, wb_ref[...]) - values
        misfit[here, :width] = e
        e2 = halves(e)
        hb = two(nt, e2, wb_ref[...])
        misfit[here, width:] = hb
        pltpu.make_async_copy(misfit.at[here], kept.at[here], sem_m.at[j]).start()
        g_ref[:, 2 * width :] += three(tn, hidden, e2)
        slope = sg * (1.0 + u * (1.0 - sg))
        g_ref[:, :width] += two_right(tn, keys, halves(hb * w * slope))
        g_ref[:, width : 2 * width] += two_right(tn, keys, halves(hb * act))

    ga = g_ref[:, : 2 * width] * gain
    g_ref[:, : 2 * width] = ga
    gb = g_ref[:, 2 * width :]
    sq_ref[...] = jnp.zeros_like(sq_ref) + (jnp.sum(ga * ga) + jnp.sum(gb * gb))
    for j in range(count):
        here = part(j, rows)
        pltpu.make_async_copy(misfit.at[here], kept.at[here], sem_m.at[j]).wait()


def call_gradient(slots, gain, wa, wb):
    count, (rows, columns) = len(slots), slots[0].shape
    width = wb.shape[0]
    return call(
        partial(gradient_kernel, count),
        "gradient",
        13,
        rows * count,
        (shape_of(width, 3 * width), shape_of(8, 128), shape_of(count * rows, 2 * width)),
        [vmem_spec(), vmem_spec(), any_spec()],
        [(x, any_spec()) for x in slots]
        + [(gain, smem_spec()), (wa, vmem_spec()), (wb, vmem_spec())],
        held_rows(count, rows, columns, bf16) + held_rows(count, rows, 2 * width, f32),
    )


def pull_query_kernel(opening, entries, *refs):
    slots, own, other = refs[:2], refs[2:4], refs[4:6]
    if opening:
        g_all, sum0, sum1, wa_ref, wb_ref, acc_ref, uh, ul, dq0, dq1 = refs[6:16]
    else:
        g_all, old, uh, ul, acc_ref, p_ref, mh, ml = refs[6:14]
    held, sem_q, left, sem_l, right, sem_r, g_ref, sem_g, sem_a = refs[-9:]
    width, rows = held.shape[1], slots[0].shape[0]
    both_in, gate, up, down = (
        slice(0, 2 * width),
        slice(0, width),
        slice(width, 2 * width),
        slice(2 * width, 3 * width),
    )
    waits = [
        fetch([block.at[:, down] for block in slots], held, sem_q),
        fetch(own, left, sem_l),
        fetch(other, right, sem_r),
    ]
    g_wait = fetch([g_all], g_ref, sem_g)
    if opening:
        g_wait(0)
        _, scale = scale_of((sum0, sum1), entries)
        rate = inner_rate / scale
        for w_ref, place in ((wa_ref, both_in), (wb_ref, down)):
            uh[:, place], ul[:, place] = halves(w_ref[...].astype(f32) - g_ref[:, place] * rate)
        acc_ref[...] = jnp.zeros_like(acc_ref)
    else:
        a_wait = fetch([old], acc_ref, sem_a)

    @pl.loop(0, 2)
    def _(j):
        for wait in waits:
            wait(j)
        here = part(j, rows)
        queries = held[here]
        d_out = halves(left[here] + right[here])
        mixed = two_right(nn, queries, (uh[:, both_in], ul[:, both_in]))
        u, w = mixed[:, :width], mixed[:, width:]
        sg = sigmoid(u)
        act = u * sg
        hb = three(nt, d_out, (uh[:, down], ul[:, down]))
        if not opening:

            @pl.when(j == 0)
            def _():
                a_wait(0)

        acc_ref[:, down] += three(tn, halves(act * w), d_out)
        slope = sg * (1.0 + u * (1.0 - sg))
        ub = halves(hb * w * slope)
        wbar = halves(hb * act)
        acc_ref[:, gate] += two_right(tn, queries, ub)
        acc_ref[:, up] += two_right(tn, queries, wbar)
        if not opening:
            for m_ref, gate_part, up_part in ((mh, ub[0], wbar[0]), (ml, ub[1], wbar[1])):
                m_ref[here, :width] = gate_part
                m_ref[here, width:] = up_part
            return
        back = three(nt, ub, (uh[:, gate], ul[:, gate])) + three(
            nt, wbar, (uh[:, up], ul[:, up])
        )
        for k, dq_ref in enumerate((dq0, dq1)):

            @pl.when(j == k)
            def _():
                dq_ref[...] = back.astype(bf16)

    if not opening:
        g_wait(0)
        p_ref[...] = jnp.zeros_like(p_ref) + jnp.sum(g_ref[...] * acc_ref[...])


def query_grad_kernel(mh, ml, uh, ul, *dqs):
    width = uh.shape[0]
    rows = mh.shape[0] // 2
    both_in = slice(0, 2 * width)
    for k, dq_ref in enumerate(dqs):
        here = slice(k * rows, (k + 1) * rows)
        back = three(nt, (mh[here], ml[here]), (uh[:, both_in], ul[:, both_in]))
        dq_ref[...] = back.astype(bf16)


def call_query_grad(mh, ml, uh, ul):
    rows, width = mh.shape[0] // 2, uh.shape[0]
    return call(
        query_grad_kernel,
        "query_grad",
        6,
        2 * rows,
        (shape_of(rows, width, dtype=bf16),) * 2,
        [vmem_spec()] * 2,
        [(x, vmem_spec()) for x in (mh, ml, uh, ul)],
        [],
    )


def call_pull_query(entries, slots, own, other, streams, more, opening):
    rows, width = slots[0].shape[0], slots[0].shape[1] // 3
    whole = shape_of(width, 3 * width)
    half = shape_of(width, 3 * width, dtype=bf16)
    dq = shape_of(rows, width, dtype=bf16)
    mixed = shape_of(2 * rows, 2 * width, dtype=bf16)
    outs = (whole, half, half, dq, dq) if opening else (whole, shape_of(8, 128), mixed, mixed)
    return call(
        partial(pull_query_kernel, opening, entries),
        "query_pull",
        20,
        rows * 2,
        outs,
        [vmem_spec()] * len(outs),
        [(x, any_spec()) for x in (*slots, *own, *other, *streams)]
        + [(x, vmem_spec()) for x in more],
        held_rows(2, rows, width, bf16)
        + held_rows(2, rows, width, f32)
        + held_rows(2, rows, width, f32)
        + held_rows(1, width, 3 * width, f32)
        + [pltpu.SemaphoreType.DMA((1,))],
    )


def pull_key_kernel(entries, blocks, *refs):
    count = len(blocks)
    slots, refs = refs[:count], refs[count:]
    kept, gain_ref, wa_ref, wb_ref = refs[:4]
    sum0, sum1, dot0, dot1, g_ref, du_ref = refs[4:10]
    out, scratch = refs[10 : 10 + count], refs[10 + count :]
    held, sem_k, kept_held, sem_e, dh, dl = scratch
    width, rows = wb_ref.shape[0], slots[0].shape[0]
    waits = [
        fetch(slots, held, sem_k),
        fetch([kept.at[part(block, rows)] for block in blocks], kept_held, sem_e),
    ]
    gain = gain_ref[0]
    rms, scale = scale_of((sum0, sum1), entries)
    pull = (dot0[0:1, 0:1] + dot1[0:1, 0:1]) / (scale * scale * entries * rms)
    dh[...], dl[...] = halves((du_ref[...] * (1.0 / scale) - g_ref[...] * pull) * (-inner_rate))
    both_in, gate, up, down = (
        slice(0, 2 * width),
        slice(0, width),
        slice(width, 2 * width),
        slice(2 * width, 3 * width),
    )

    @pl.loop(0, count)
    def _(j):
        for wait in waits:
            wait(j)
        here = part(j, rows)
        keys = held[here, :width]
        mixed = nn(keys, wa_ref[...]) * gain
        moved = two_right(nn, keys, (dh[:, both_in], dl[:, both_in])) * gain
        u, w = mixed[:, :width], mixed[:, width:]
        du, dw = moved[:, :width], moved[:, width:]
        sg = sigmoid(u)
        act = u * sg
        rest = 1.0 - sg
        slope = sg * (1.0 + u * rest)
        bend = sg * rest * (2.0 + u * (rest - sg))
        db = (dh[:, down], dl[:, down])
        shift = two(nn, halves(slope * du * w + act * dw), wb_ref[...]) + three(
            nn, halves(act * w), db
        )
        back = two(nt, halves(shift), wb_ref[...]) + three(
            nt, halves(kept_held[here, :width]), db
        )
        hb = kept_held[here, width:]
        ub = halves(back * w * slope + hb * (bend * du * w + slope * dw))
        wbar = halves(back * act + hb * slope * du)
        ut = halves(hb * slope * w)
        wt = halves(hb * act)
        grad = (
            two(nt, ub, wa_ref[:, :width])
            + two(nt, wbar, wa_ref[:, width:])
            + three(nt, ut, (dh[:, gate], dl[:, gate]))
            + three(nt, wt, (dh[:, up], dl[:, up]))
        )
        for k, out_ref in enumerate(out):

            @pl.when(j == k)
            def _():
                out_ref[:, :width] = (grad * gain).astype(bf16)
                out_ref[:, width:] = (-shift).astype(bf16)


def call_pull_key(blocks, entries, slots, kept, gain, wa, wb, terms):
    count, (rows, columns) = len(blocks), slots[0].shape
    width = wb.shape[0]
    return call(
        partial(pull_key_kernel, entries, blocks),
        "key_pull",
        26,
        rows * count,
        (shape_of(rows, 2 * width, dtype=bf16),) * count,
        [vmem_spec()] * count,
        [(slots[block], any_spec()) for block in blocks]
        + [(kept, any_spec()), (gain, smem_spec()), (wa, vmem_spec()), (wb, vmem_spec())]
        + [(x, vmem_spec()) for x in terms],
        held_rows(count, rows, columns, bf16)
        + held_rows(count, rows, 2 * width, f32)
        + [pltpu.VMEM((width, 3 * width), bf16)] * 2,
    )


def four_line(queries, keys, values, fast_in, fast_out, key_gain, out_proj, grad_out):
    toks, heads = 4, lax.axis_size("head")
    low, high = 1, 2
    width = fast_out.shape[1]
    entries = float(heads * (fast_in.shape[1] * fast_in.shape[2] + width * fast_out.shape[2]))
    place, head = lax.axis_index("tok"), lax.axis_index("head")
    core = lax.rem(head, 2)
    line, mirror = (1, 0, 2, 3), (2, 3, 1, 0)
    both = ("tok", "head")
    tie = lax.optimization_barrier

    def flat(t, h):
        return t * heads + h

    def root(h):
        return high if h % 2 else low

    def order(h):
        return mirror if h % 2 else line

    def to_root(j):
        return [(flat(order(h)[j], h), flat(root(h), h)) for h in range(heads)]

    def home(value, j):
        return lax.ppermute(value, both, [(b, a) for a, b in to_root(j)])

    is_root = place == jnp.where(core == 0, low, high)
    wa, wb = fast_in[0], fast_out[0]
    rows_in = jnp.concatenate([keys, values, queries], axis=1)
    slots = [rows_in] + [lax.ppermute(rows_in, both, to_root(j)) for j in range(1, toks)]

    group, half = lax.axis_index("groups"), out_proj.shape[0] // 2
    far_half = lax.ppermute(
        lax.dynamic_slice_in_dim(out_proj, group * half, half, axis=0),
        "tok",
        [(0, low), (3, high)],
    )
    quarter = grad_out.shape[1] // 4

    def columns(array, which, half_is_low):
        index = jnp.where(half_is_low, 1 - which, 2 + which)
        return lax.dynamic_slice_in_dim(array, index * quarter, quarter, axis=1)

    def piece(array, j):
        return lax.ppermute(
            columns(array, core, place == line[j]), "tok", [(line[j], low), (mirror[j], high)]
        )

    def swap_cores(value):
        return lax.ppermute(value, "head", [(h, h ^ 1) for h in range(heads)])

    piece2 = piece(grad_out, 2)
    later, far_half, piece2, *slots = tie((grad_out, far_half, piece2, *slots))
    far_other = lax.ppermute(far_half, "groups", [(0, 1), (1, 0)])

    def exchange(value, pairs, step_pairs, beside=None):
        more = lax.ppermute(value, both, pairs)
        if beside is not None:
            outs, more = tie((beside(), more))
        value = value + more
        step = 2
        while True:
            more = lax.ppermute(value, both, step_pairs(step))
            step *= 2
            if step >= heads:
                return (value, more) if beside is None else (value, more, outs)
            value = value + more

    over = [
        (flat(high, h), flat(low, h)) if h % 2 == 0 else (flat(low, h), flat(high, h))
        for h in range(heads)
    ]
    root_pairs = [(flat(root(h), h), flat(root(h ^ 1), h ^ 1)) for h in range(heads)]

    def root_steps(step):
        return [(flat(root(h), h), flat(root(h), h ^ step)) for h in range(heads)]

    at_low = place <= low
    piece3 = piece(later, 3)
    piece1 = piece(later, 1)
    g, squares, kept = call_gradient(slots, key_gain, wa, wb)
    g, squares, far_half, far_other, piece2, mine0, theirs0 = tie(
        (
            g,
            squares,
            far_half,
            far_other,
            piece2,
            columns(later, core, at_low),
            columns(later, 1 - core, at_low),
        )
    )

    far = jnp.where(
        group == 0,
        jnp.concatenate([far_half, far_other], axis=0),
        jnp.concatenate([far_other, far_half], axis=0),
    )
    w_mine = jnp.where(core == 0, out_proj, far)
    w_theirs = jnp.where(core == 0, far, out_proj)

    def product(mine, theirs):
        return nt(mine, w_mine) + nt(theirs, w_theirs)

    own0 = product(mine0, theirs0)
    other2 = lax.ppermute(own0, both, over)
    own2 = product(piece2, swap_cores(piece2))
    other0 = lax.ppermute(own2, both, over)
    *sums, (own0, own2) = exchange(squares, root_pairs, root_steps, lambda: (own0, own2))
    piece3, piece1, own0 = tie((piece3, piece1, own0))
    own3 = product(piece3, swap_cores(piece3))
    other1 = lax.ppermute(own3, both, over)
    own1 = product(piece1, swap_cores(piece1))
    other3 = lax.ppermute(own1, both, over)
    own3, own1, *sums = tie((own3, own1, *sums))
    acc, uh, ul, dq0, dq2 = call_pull_query(
        entries, slots[0::2], (own0, own2), (other0, other2), (g,), (*sums, wa, wb), True
    )
    other1, other3, acc, uh, ul, dq2 = tie((other1, other3, acc, uh, ul, dq2))

    du, dots, mh, ml = call_pull_query(
        entries, slots[1::2], (own1, own3), (other1, other3), (g, acc), (uh, ul), False
    )
    du, dots, mh, ml = tie((du, dots, mh, ml))

    *dots, (dq1, dq3) = exchange(
        dots, root_pairs, root_steps, lambda: call_query_grad(mh, ml, uh, ul)
    )
    du, dq1, dq3, *dots = tie((du, dq1, dq3, *dots))

    terms = (*sums, *dots, g, du)
    dq1, dq2, dq3 = home(dq1, 1), home(dq2, 2), home(dq3, 3)
    out3, out2 = call_pull_key((3, 2), entries, slots, kept, key_gain, wa, wb, terms)
    out3, out2, dq1, dq2, dq3, *terms = tie((out3, out2, dq1, dq2, dq3, *terms))

    out3, out2 = home(out3, 3), home(out2, 2)
    (out1,) = call_pull_key((1,), entries, slots, kept, key_gain, wa, wb, terms)
    d_queries = jnp.where(is_root, dq0, dq1 + dq2 + dq3)
    out3, out2, out1, d_queries, *terms = tie((out3, out2, out1, d_queries, *terms))

    out1 = home(out1, 1)
    (out0,) = call_pull_key((0,), entries, slots, kept, key_gain, wa, wb, terms)
    pair = jnp.where(is_root, out0, out1 + out2 + out3)
    return d_queries, pair[:, :width], pair[:, width:]


def per_device(*arrays):
    fits = lax.axis_size("tok") == 4 and lax.axis_size("head") >= 4 and lax.axis_size("groups") == 2
    return (four_line if fits else any_line)(*arrays)


def solution(mesh):
    rows = P(("groups", "tok"), "head")
    return jax.shard_map(
        per_device,
        mesh=mesh,
        in_specs=(
            rows,
            rows,
            rows,
            P("head", None, None),
            P("head", None, None),
            P("head"),
            P("head", "tok"),
            P(("groups", "tok"), None),
        ),
        out_specs=(rows, rows, rows),
        check_vma=False,
    )
```
